32 devices in a mesh: sp: 2 (over x), dp: 16 (over z, y, core).
Axes of the slice: x: 2, y: 2, z: 4, core: 2. Of those that a mesh axis runs over, the one named last changes fastest.
Arguments:
- inputs: bfloat16 [32, 8, 8, 8, 128], P('dp', 'sp'), may hold values from -6 to 6
- cotangent: bfloat16 [32, 8, 8, 8, 128], P('dp', 'sp'), may hold values from -6 to 6
- w_conv: bfloat16 [3456, 128], replicated, may hold values from -0.109375 to 0.109375
- w_down: bfloat16 [1024, 256], replicated, may hold values from -0.1875 to 0.1875
- w_up: bfloat16 [2048, 128], replicated, may hold values from -0.375 to 0.375
Outputs:
- grad_input: bfloat16 [32, 8, 8, 8, 128], P('dp', 'sp')
- weight_grads: float32 [966656], P('dp')
The draws below stay inside these ranges and needn't reach their ends.
All inputs are finite; a program needn't handle non-finite values.
Results may differ from the reference program's by a relative error of at most 0.017.
Values may be sent and summed in bfloat16 or wider, within the bound.
No kernel may reach another device: no remote copies, remote signals or barrier semaphores. Data moves between devices by JAX's collectives and lax.ppermute only.
A program may use at most 64 MiB of HBM per device.

```python
import jax
import jax.numpy as jnp
from jax import lax

C1 = 128
C2 = 256
S = 8
CROPS = 32


def with_spikes(array, rng, source, target, parts, factor):
    def block_of(axis_at):
        return (jnp.arange(array.shape[axis_at]) // (array.shape[axis_at] // parts)).reshape((-1,) + (1,) * (array.ndim - 1 - axis_at))

    near = jax.random.permutation(rng, parts)[block_of(target)]
    second = (block_of(target) + parts // 2) % parts
    return jnp.where((block_of(source) == near) | (block_of(source) == second), factor * array, array)


def block_levels(own_key, shape, cuts, low, high):
    gain, own = 1.0, jax.random.fold_in(own_key, 6)
    for position, parts in cuts:
        heights = jnp.exp(jax.random.uniform(jax.random.fold_in(own, position), (parts,), jnp.float32, low / len(cuts), high / len(cuts)))
        gain = gain * jnp.repeat(heights, shape[position] // parts).reshape([-1 if axis == position else 1 for axis in range(len(shape))])
    return gain


def normal_values(key, shape, deviation, most, split=(), held_as=jnp.bfloat16):
    factor_of = block_levels(key, shape, split, -0.22, 0.18) if split else 1.0
    array = jax.random.normal(key, shape, jnp.float32) * deviation * factor_of
    return jnp.minimum(jnp.maximum(array, -most), most).astype(held_as)


def bell_draw_with(own_key, dims, scale, limit, split, heavy, dtype=jnp.bfloat16):
    result = scale * jax.random.normal(own_key, dims, jnp.float32)
    if split:
        result = result * block_levels(own_key, dims, split, -0.22, 0.18)
    return jnp.clip(with_spikes(result, jax.random.fold_in(own_key, 3), *heavy), -limit, limit).astype(dtype)


def setup_inputs(seed: int = 0) -> dict:
    keys = jax.random.split(jax.random.key(seed), 6)
    return {
        "inputs": bell_draw_with(keys[0], (CROPS, S, S, S, C1), 1.0, 6.0, ((0, 16), (1, 2)), (0, 4, 16, 2.0)),
        "cotangent": normal_values(keys[1], (CROPS, S, S, S, C1), 1.0, 6.0, ((0, 16), (1, 2))),
        "w_conv": normal_values(keys[2], (27 * C1, C1), (27 * C1) ** -0.5, 0.109375),
        "w_down": normal_values(keys[3], (8 * C1, C2), (8 * C1) ** -0.5, 0.1875),
        "w_up": normal_values(keys[4], (8 * C2, C1), C2 ** -0.5, 0.375),
    }


def silu_slope(pre_act):
    sigmoid_value = jax.nn.sigmoid(pre_act)
    return sigmoid_value * (1.0 + pre_act * (1.0 - sigmoid_value))

def unfold_taps(padded):
    first_size = padded.shape[1] - 2
    second_size = padded.shape[2] - 2
    third_size = padded.shape[3] - 2
    pieces = [padded[:, i:i + first_size, j:j + second_size, k:k + third_size, :] for i in range(3) for j in range(3) for k in range(3)]
    stacked = jnp.concatenate(pieces, axis=-1)
    return stacked.reshape(-1, stacked.shape[-1])

def to_blocks(volume):
    shape = volume.shape
    folded = volume.reshape(shape[0], shape[1] // 2, 2, shape[2] // 2, 2, shape[3] // 2, 2, shape[4])
    folded = folded.transpose(0, 1, 3, 5, 2, 4, 6, 7)
    return folded.reshape(-1, 8 * shape[4])

def from_blocks(blocked, shape):
    folded = blocked.reshape(shape[0], shape[1] // 2, shape[2] // 2, shape[3] // 2, 2, 2, 2, shape[4])
    folded = folded.transpose(0, 1, 4, 2, 5, 3, 6, 7)
    return folded.reshape(shape)

def flip_taps(w_conv):
    width_in = w_conv.shape[1]
    return w_conv.reshape(27, width_in, width_in)[::-1].transpose(0, 2, 1).reshape(27 * width_in, width_in)

def deep_level(hidden, upstream, w_down, w_up):
    width_in = hidden.shape[-1]
    width_deep = w_down.shape[1]
    hid_blocks = to_blocks(hidden)
    up_blocks = to_blocks(upstream)
    pre_deep = jnp.dot(hid_blocks, w_down, preferred_element_type=jnp.float32)
    deep_act = jax.nn.silu(pre_deep).astype(jnp.bfloat16)
    w_up_back = w_up.reshape(8, width_deep, width_in).transpose(0, 2, 1).reshape(8 * width_in, width_deep)
    grad_act = jnp.dot(up_blocks, w_up_back, preferred_element_type=jnp.float32)
    grad_up = lax.dot_general(deep_act, up_blocks, (((0,), (0,)), ((), ())), preferred_element_type=jnp.float32)
    grad_up = grad_up.reshape(width_deep, 8, width_in).transpose(1, 0, 2).reshape(8 * width_deep, width_in)
    grad_deep = (grad_act * silu_slope(pre_deep)).astype(jnp.bfloat16)
    grad_down = lax.dot_general(hid_blocks, grad_deep, (((0,), (0,)), ((), ())), preferred_element_type=jnp.float32)
    back_blocks = jnp.dot(grad_deep, w_down.T, preferred_element_type=jnp.float32).astype(jnp.bfloat16)
    return (grad_down, grad_up, from_blocks(back_blocks, hidden.shape))

def reference(inputs, cotangent, w_conv, w_down, w_up):
    width_in = w_conv.shape[1]
    w_flip = flip_taps(w_conv)

    def one_crop(carry, pair):
        volume = pair[0][None]
        upstream = pair[1][None]
        padded = jnp.pad(volume, ((0, 0), (1, 1), (1, 1), (1, 1), (0, 0)))
        columns = unfold_taps(padded)
        pre_conv = jnp.dot(columns, w_conv, preferred_element_type=jnp.float32)
        hidden = jax.nn.silu(pre_conv).astype(jnp.bfloat16).reshape(volume.shape)
        grad_down, grad_up, back_down = deep_level(hidden, upstream, w_down, w_up)
        summed = upstream.astype(jnp.float32).reshape(-1, width_in) + back_down.astype(jnp.float32).reshape(-1, width_in)
        grad_pre = (summed * silu_slope(pre_conv)).astype(jnp.bfloat16)
        grad_conv = lax.dot_general(columns, grad_pre, (((0,), (0,)), ((), ())), preferred_element_type=jnp.float32)
        grad_pad = jnp.pad(grad_pre.reshape(volume.shape), ((0, 0), (1, 1), (1, 1), (1, 1), (0, 0)))
        grad_input = jnp.dot(unfold_taps(grad_pad), w_flip, preferred_element_type=jnp.float32).astype(jnp.bfloat16)
        new_carry = (carry[0] + grad_conv, carry[1] + grad_down, carry[2] + grad_up)
        return (new_carry, grad_input.reshape(volume.shape[1:]))
    start = (jnp.zeros(w_conv.shape, jnp.float32), jnp.zeros(w_down.shape, jnp.float32), jnp.zeros(w_up.shape, jnp.float32))
    totals, grad_input = lax.scan(one_crop, start, (inputs, cotangent))
    norm_factor = 1.0 / jnp.sqrt(jnp.float32(CROPS * S * S * S))
    weight_grads = jnp.concatenate([totals[0].reshape(-1), totals[1].reshape(-1), totals[2].reshape(-1)]) * norm_factor
    return (grad_input, weight_grads)
```

```python
import jax
import jax.numpy as jnp
from jax import lax
from jax.sharding import PartitionSpec as P


def extended(cells, sides, width):
    for axis, dim in sides:
        count = lax.axis_size(axis)
        ends = count - 1
        head = lax.slice_in_dim(cells, 0, width, axis=dim)
        tail = lax.slice_in_dim(cells, cells.shape[dim] - width, cells.shape[dim], axis=dim)
        cells = jnp.concatenate(
            [
                lax.ppermute(tail, axis, [(i, (i + 1) % count) for i in range(ends)]),
                cells,
                lax.ppermute(head, axis, [((i + 1) % count, i) for i in range(ends)]),
            ],
            axis=dim,
        )
    return cells


def silu_slope(pre_act):
    sigmoid_value = jax.nn.sigmoid(pre_act)
    return sigmoid_value * (1.0 + pre_act * (1.0 - sigmoid_value))


def unfold_taps(padded):
    first_size = padded.shape[1] - 2
    second_size = padded.shape[2] - 2
    third_size = padded.shape[3] - 2
    pieces = [
        padded[:, i : i + first_size, j : j + second_size, k : k + third_size, :]
        for i in range(3)
        for j in range(3)
        for k in range(3)
    ]
    stacked = jnp.concatenate(pieces, axis=-1)
    return stacked.reshape(-1, stacked.shape[-1])


def to_blocks(volume):
    shape = volume.shape
    folded = volume.reshape(
        shape[0], shape[1] // 2, 2, shape[2] // 2, 2, shape[3] // 2, 2, shape[4]
    )
    folded = folded.transpose(0, 1, 3, 5, 2, 4, 6, 7)
    return folded.reshape(-1, 8 * shape[4])


def from_blocks(blocked, shape):
    folded = blocked.reshape(
        shape[0], shape[1] // 2, shape[2] // 2, shape[3] // 2, 2, 2, 2, shape[4]
    )
    folded = folded.transpose(0, 1, 4, 2, 5, 3, 6, 7)
    return folded.reshape(shape)


def flip_taps(w_conv):
    width_in = w_conv.shape[1]
    return (
        w_conv.reshape(27, width_in, width_in)[::-1]
        .transpose(0, 2, 1)
        .reshape(27 * width_in, width_in)
    )


def deep_level(hidden, upstream, w_down, w_up):
    width_in = hidden.shape[-1]
    width_deep = w_down.shape[1]
    hid_blocks = to_blocks(hidden)
    up_blocks = to_blocks(upstream)
    pre_deep = jnp.dot(hid_blocks, w_down, preferred_element_type=jnp.float32)
    deep_act = jax.nn.silu(pre_deep).astype(jnp.bfloat16)
    w_up_back = (
        w_up.reshape(8, width_deep, width_in).transpose(0, 2, 1).reshape(8 * width_in, width_deep)
    )
    grad_act = jnp.dot(up_blocks, w_up_back, preferred_element_type=jnp.float32)
    grad_up = lax.dot_general(
        deep_act, up_blocks, (((0,), (0,)), ((), ())), preferred_element_type=jnp.float32
    )
    grad_up = (
        grad_up.reshape(width_deep, 8, width_in)
        .transpose(1, 0, 2)
        .reshape(8 * width_deep, width_in)
    )
    grad_deep = (grad_act * silu_slope(pre_deep)).astype(jnp.bfloat16)
    grad_down = lax.dot_general(
        hid_blocks, grad_deep, (((0,), (0,)), ((), ())), preferred_element_type=jnp.float32
    )
    back_blocks = jnp.dot(grad_deep, w_down.T, preferred_element_type=jnp.float32).astype(
        jnp.bfloat16
    )
    return (grad_down, grad_up, from_blocks(back_blocks, hidden.shape))


def per_device(inputs, cotangent, w_conv, w_down, w_up):
    width_in = w_conv.shape[1]
    edge_pad = ((0, 0), (0, 0), (1, 1), (1, 1), (0, 0))
    slab_in = extended(inputs, (("sp", 1),), 1)
    columns = unfold_taps(jnp.pad(slab_in, edge_pad))
    pre_conv = jnp.dot(columns, w_conv, preferred_element_type=jnp.float32)
    hidden = jax.nn.silu(pre_conv).astype(jnp.bfloat16).reshape(inputs.shape)
    hidden_crops, upstream_crops = (
        lax.all_to_all(hidden, "sp", split_axis=0, concat_axis=1, tiled=True),
        lax.all_to_all(cotangent, "sp", split_axis=0, concat_axis=1, tiled=True),
    )
    grad_down, grad_up, back_down = deep_level(hidden_crops, upstream_crops, w_down, w_up)
    back_slab = lax.all_to_all(back_down, "sp", split_axis=1, concat_axis=0, tiled=True)
    summed = cotangent.astype(jnp.float32).reshape(-1, width_in) + back_slab.astype(
        jnp.float32
    ).reshape(-1, width_in)
    grad_pre = (summed * silu_slope(pre_conv)).astype(jnp.bfloat16)
    grad_conv = lax.dot_general(
        columns, grad_pre, (((0,), (0,)), ((), ())), preferred_element_type=jnp.float32
    )
    padded_grad = extended(grad_pre.reshape(inputs.shape), (("sp", 1),), 1)
    grad_input = jnp.dot(
        unfold_taps(jnp.pad(padded_grad, edge_pad)),
        flip_taps(w_conv),
        preferred_element_type=jnp.float32,
    )
    grad_input = grad_input.astype(jnp.bfloat16).reshape(inputs.shape)
    local_sums = jnp.concatenate(
        [grad_conv.reshape(-1), grad_down.reshape(-1), grad_up.reshape(-1)]
    )
    within_group = lax.psum(local_sums.astype(jnp.bfloat16), "sp").astype(jnp.float32)
    grad_share = lax.psum_scatter(within_group, "dp", scatter_dimension=0, tiled=True)
    edge_cells = inputs.shape[2]
    crop_total = inputs.shape[0] * lax.axis_size("dp")
    norm_factor = 1.0 / jnp.sqrt(jnp.float32(crop_total * edge_cells * edge_cells * edge_cells))
    return (grad_input, grad_share * norm_factor)


def swap_x(value):
    return lax.ppermute(value, "sp", [(0, 1), (1, 0)])


def swap_dp(value, mask):
    return lax.ppermute(value, "dp", [(i, i ^ mask) for i in range(16)])


def pick(value, dim, index):
    return lax.dynamic_index_in_dim(value, index, dim, keepdims=False)


def sum_shares(mine, passed, scale):
    at = lax.axis_index("dp")
    side = lax.axis_index("sp")
    row, near, far = (at >> 1) & 1, (at >> 2) & 1, (at >> 3) & 1

    def chip_sum(z, y):
        return pick(pick(mine, 1, z), 1, y).astype(jnp.float32) + pick(
            pick(passed, 1, z), 1, y
        ).astype(jnp.float32)

    diagonal = swap_dp(chip_sum(1 - near, 1 - row).astype(jnp.bfloat16), 6)
    along_y = swap_dp(chip_sum(near, 1 - row).astype(jnp.bfloat16), 2)
    along_z = swap_dp(chip_sum(1 - near, row).astype(jnp.bfloat16), 4)
    square = (
        chip_sum(near, row)
        + along_y.astype(jnp.float32)
        + along_z.astype(jnp.float32)
        + diagonal.astype(jnp.float32)
    )
    across = swap_dp(pick(square, 0, 1 - far).astype(jnp.bfloat16), 8)
    total = (pick(square, 0, far) + across.astype(jnp.float32)).astype(jnp.bfloat16)
    other = swap_x(total)
    low = jnp.where(side == 0, total, other)
    high = jnp.where(side == 0, other, total)
    return low.astype(jnp.float32) * scale, high.astype(jnp.float32) * scale


def per_device_pairs(inputs, cotangent, w_conv, w_down, w_up):
    width_in = w_conv.shape[1]
    side = lax.axis_index("sp")
    other_in = swap_x(inputs)
    other_up = swap_x(cotangent)

    def whole(own, other):
        low = jnp.where(side == 0, own, other)
        high = jnp.where(side == 0, other, own)
        return jnp.concatenate([low, high], axis=1)

    volume = whole(inputs, other_in)
    upstream = whole(cotangent, other_up)
    edge_pad = ((0, 0), (1, 1), (1, 1), (1, 1), (0, 0))
    columns = unfold_taps(jnp.pad(volume, edge_pad))
    pre_conv = jnp.dot(columns, w_conv, preferred_element_type=jnp.float32)
    hidden = jax.nn.silu(pre_conv).astype(jnp.bfloat16).reshape(volume.shape)
    grad_down, grad_up, back_down = deep_level(hidden, upstream, w_down, w_up)
    summed = upstream.astype(jnp.float32).reshape(-1, width_in) + back_down.astype(
        jnp.float32
    ).reshape(-1, width_in)
    grad_pre = (summed * silu_slope(pre_conv)).astype(jnp.bfloat16)
    grad_conv = lax.dot_general(
        columns, grad_pre, (((0,), (0,)), ((), ())), preferred_element_type=jnp.float32
    )
    padded_grad = jnp.pad(grad_pre.reshape(volume.shape), edge_pad)
    slab = lax.dynamic_slice_in_dim(
        padded_grad, side * inputs.shape[1], inputs.shape[1] + 2, axis=1
    )
    grad_input = jnp.dot(
        unfold_taps(slab), flip_taps(w_conv), preferred_element_type=jnp.float32
    )
    grad_input = grad_input.astype(jnp.bfloat16).reshape(inputs.shape)

    lanes = 128
    rows = jnp.concatenate(
        [part.reshape(-1, lanes) for part in (grad_conv, grad_down, grad_up)]
    ).astype(jnp.bfloat16)
    shares = rows.reshape(16, -1, lanes)
    per_share = shares.shape[1]
    half = -(-per_share // 32) * 16
    part = lax.dynamic_slice_in_dim(shares, side * (per_share - half), half, axis=1)
    part = part.reshape(2, 2, 2, 2, half, lanes)
    core = lax.axis_index("dp") & 1
    passed = swap_dp(pick(part, 3, 1 - core), 1)
    crop_total = inputs.shape[0] * lax.axis_size("dp")
    scale = 1.0 / jnp.sqrt(jnp.float32(crop_total * inputs.shape[2] ** 3))
    low, high = sum_shares(pick(part, 3, core), passed, scale)
    grad_share = jnp.concatenate([low, high[2 * half - per_share :]]).reshape(-1)
    return (grad_input, grad_share)


def solution(mesh):
    pairs = dict(mesh.shape) == {"sp": 2, "dp": 16}
    return jax.shard_map(
        per_device_pairs if pairs else per_device,
        mesh=mesh,
        in_specs=(P("dp", "sp", None, None, None), P("dp", "sp", None, None, None), P(), P(), P()),
        out_specs=(P("dp", "sp", None, None, None), P("dp")),
        check_vma=False,
    )
```

```python
import jax
import jax.numpy as jnp
from jax import lax
from jax.experimental import pallas as pl
from jax.experimental.pallas import tpu as pltpu
from jax.sharding import PartitionSpec as P


def extended(cells, sides, width):
    for axis, dim in sides:
        count = lax.axis_size(axis)
        ends = count - 1
        head = lax.slice_in_dim(cells, 0, width, axis=dim)
        tail = lax.slice_in_dim(cells, cells.shape[dim] - width, cells.shape[dim], axis=dim)
        cells = jnp.concatenate(
            [
                lax.ppermute(tail, axis, [(i, (i + 1) % count) for i in range(ends)]),
                cells,
                lax.ppermute(head, axis, [((i + 1) % count, i) for i in range(ends)]),
            ],
            axis=dim,
        )
    return cells


def silu_slope(pre_act):
    sigmoid_value = jax.nn.sigmoid(pre_act)
    return sigmoid_value * (1.0 + pre_act * (1.0 - sigmoid_value))


def unfold_taps(padded):
    first_size = padded.shape[1] - 2
    second_size = padded.shape[2] - 2
    third_size = padded.shape[3] - 2
    pieces = [
        padded[:, i : i + first_size, j : j + second_size, k : k + third_size, :]
        for i in range(3)
        for j in range(3)
        for k in range(3)
    ]
    stacked = jnp.concatenate(pieces, axis=-1)
    return stacked.reshape(-1, stacked.shape[-1])


def to_blocks(volume):
    shape = volume.shape
    folded = volume.reshape(
        shape[0], shape[1] // 2, 2, shape[2] // 2, 2, shape[3] // 2, 2, shape[4]
    )
    folded = folded.transpose(0, 1, 3, 5, 2, 4, 6, 7)
    return folded.reshape(-1, 8 * shape[4])


def from_blocks(blocked, shape):
    folded = blocked.reshape(
        shape[0], shape[1] // 2, shape[2] // 2, shape[3] // 2, 2, 2, 2, shape[4]
    )
    folded = folded.transpose(0, 1, 4, 2, 5, 3, 6, 7)
    return folded.reshape(shape)


def flip_taps(w_conv):
    width_in = w_conv.shape[1]
    return (
        w_conv.reshape(27, width_in, width_in)[::-1]
        .transpose(0, 2, 1)
        .reshape(27 * width_in, width_in)
    )


def deep_level(hidden, upstream, w_down, w_up):
    width_in = hidden.shape[-1]
    width_deep = w_down.shape[1]
    hid_blocks = to_blocks(hidden)
    up_blocks = to_blocks(upstream)
    pre_deep = jnp.dot(hid_blocks, w_down, preferred_element_type=jnp.float32)
    deep_act = jax.nn.silu(pre_deep).astype(jnp.bfloat16)
    w_up_back = (
        w_up.reshape(8, width_deep, width_in).transpose(0, 2, 1).reshape(8 * width_in, width_deep)
    )
    grad_act = jnp.dot(up_blocks, w_up_back, preferred_element_type=jnp.float32)
    grad_up = lax.dot_general(
        deep_act, up_blocks, (((0,), (0,)), ((), ())), preferred_element_type=jnp.float32
    )
    grad_up = (
        grad_up.reshape(width_deep, 8, width_in)
        .transpose(1, 0, 2)
        .reshape(8 * width_deep, width_in)
    )
    grad_deep = (grad_act * silu_slope(pre_deep)).astype(jnp.bfloat16)
    grad_down = lax.dot_general(
        hid_blocks, grad_deep, (((0,), (0,)), ((), ())), preferred_element_type=jnp.float32
    )
    back_blocks = jnp.dot(grad_deep, w_down.T, preferred_element_type=jnp.float32).astype(
        jnp.bfloat16
    )
    return (grad_down, grad_up, from_blocks(back_blocks, hidden.shape))


def per_device(inputs, cotangent, w_conv, w_down, w_up):
    width_in = w_conv.shape[1]
    edge_pad = ((0, 0), (0, 0), (1, 1), (1, 1), (0, 0))
    slab_in = extended(inputs, (("sp", 1),), 1)
    columns = unfold_taps(jnp.pad(slab_in, edge_pad))
    pre_conv = jnp.dot(columns, w_conv, preferred_element_type=jnp.float32)
    hidden = jax.nn.silu(pre_conv).astype(jnp.bfloat16).reshape(inputs.shape)
    hidden_crops, upstream_crops = (
        lax.all_to_all(hidden, "sp", split_axis=0, concat_axis=1, tiled=True),
        lax.all_to_all(cotangent, "sp", split_axis=0, concat_axis=1, tiled=True),
    )
    grad_down, grad_up, back_down = deep_level(hidden_crops, upstream_crops, w_down, w_up)
    back_slab = lax.all_to_all(back_down, "sp", split_axis=1, concat_axis=0, tiled=True)
    summed = cotangent.astype(jnp.float32).reshape(-1, width_in) + back_slab.astype(
        jnp.float32
    ).reshape(-1, width_in)
    grad_pre = (summed * silu_slope(pre_conv)).astype(jnp.bfloat16)
    grad_conv = lax.dot_general(
        columns, grad_pre, (((0,), (0,)), ((), ())), preferred_element_type=jnp.float32
    )
    padded_grad = extended(grad_pre.reshape(inputs.shape), (("sp", 1),), 1)
    grad_input = jnp.dot(
        unfold_taps(jnp.pad(padded_grad, edge_pad)),
        flip_taps(w_conv),
        preferred_element_type=jnp.float32,
    )
    grad_input = grad_input.astype(jnp.bfloat16).reshape(inputs.shape)
    local_sums = jnp.concatenate(
        [grad_conv.reshape(-1), grad_down.reshape(-1), grad_up.reshape(-1)]
    )
    within_group = lax.psum(local_sums.astype(jnp.bfloat16), "sp").astype(jnp.float32)
    grad_share = lax.psum_scatter(within_group, "dp", scatter_dimension=0, tiled=True)
    edge_cells = inputs.shape[2]
    crop_total = inputs.shape[0] * lax.axis_size("dp")
    norm_factor = 1.0 / jnp.sqrt(jnp.float32(crop_total * edge_cells * edge_cells * edge_cells))
    return (grad_input, grad_share * norm_factor)


def swap_x(value):
    return lax.ppermute(value, "sp", [(0, 1), (1, 0)])


def swap_dp(value, mask):
    return lax.ppermute(value, "dp", [(i, i ^ mask) for i in range(16)])


def pick(value, dim, index):
    return lax.dynamic_index_in_dim(value, index, dim, keepdims=False)


def sum_shares(mine, passed, scale):
    at = lax.axis_index("dp")
    side = lax.axis_index("sp")
    row, near, far = (at >> 1) & 1, (at >> 2) & 1, (at >> 3) & 1

    def chip_sum(z, y):
        return pick(pick(mine, 1, z), 1, y).astype(jnp.float32) + pick(
            pick(passed, 1, z), 1, y
        ).astype(jnp.float32)

    diagonal = swap_dp(chip_sum(1 - near, 1 - row).astype(jnp.bfloat16), 6)
    along_y = swap_dp(chip_sum(near, 1 - row).astype(jnp.bfloat16), 2)
    along_z = swap_dp(chip_sum(1 - near, row).astype(jnp.bfloat16), 4)
    square = (
        chip_sum(near, row)
        + along_y.astype(jnp.float32)
        + along_z.astype(jnp.float32)
        + diagonal.astype(jnp.float32)
    )
    across = swap_dp(pick(square, 0, 1 - far).astype(jnp.bfloat16), 8)
    total = (pick(square, 0, far) + across.astype(jnp.float32)).astype(jnp.bfloat16)
    other = swap_x(total)
    low = jnp.where(side == 0, total, other)
    high = jnp.where(side == 0, other, total)
    return low.astype(jnp.float32) * scale, high.astype(jnp.float32) * scale


LANES = 128
VMEM = pl.BlockSpec(memory_space=pltpu.VMEM)


def load_crops(own_ref, other_ref, natural_ref, side):
    depth = own_ref.shape[1]
    for ref, first in ((own_ref, side * depth), (other_ref, (1 - side) * depth)):
        for crop in range(2):
            natural_ref[pl.ds(first, depth), :, 8 * crop : 8 * crop + 8, :] = ref[crop].astype(
                jnp.float32
            )


def fill_taps(taps_ref, even, odd):
    planes = even.shape[0]
    kk = lax.broadcasted_iota(jnp.int32, even.shape, 2) % 4
    before = jnp.where(kk == 0, 0.0, pltpu.roll(odd, 1, 2))
    after = jnp.where(kk == 3, 0.0, pltpu.roll(even, 7, 2))
    rows = pl.ds(1, 8)
    for tap, (low, high) in enumerate(((before, even), (even, odd), (odd, after))):
        taps_ref[1 : 1 + planes, rows, :, tap * LANES : (tap + 1) * LANES] = jnp.concatenate(
            [low, high], axis=2
        ).astype(jnp.bfloat16)


def clear_rim(taps_ref, with_planes):
    planes, rows, tile, lanes = taps_ref.shape
    row = jnp.zeros((planes, tile, lanes), jnp.bfloat16)
    taps_ref[:, 0] = row
    taps_ref[:, rows - 1] = row
    if with_planes:
        plane = jnp.zeros((rows, tile, lanes), jnp.bfloat16)
        taps_ref[0] = plane
        taps_ref[planes - 1] = plane


def across(tile):
    return jnp.concatenate(tile, axis=-1)


def forward_kernel(own_ref, other_ref, w_ref, pre_ref, turned_ref, natural_ref, taps_ref):
    side = lax.axis_index("sp")
    load_crops(own_ref, other_ref, natural_ref, side)
    even = natural_ref[:, :, pl.ds(0, 8, stride=2), :]
    odd = natural_ref[:, :, pl.ds(1, 8, stride=2), :]
    clear_rim(taps_ref, False)
    fill_taps(taps_ref, even, odd)
    wide = 3 * LANES
    planes = even.shape[0]
    size = planes * 128
    centre = taps_ref[1 : 1 + planes, 1:9, :, LANES : 2 * LANES].reshape(size, LANES)
    turned_ref[...] = centre.astype(jnp.float32).T.astype(jnp.bfloat16)
    cells = across(
        [taps_ref[1 : 1 + planes, j : j + 8].reshape(size, wide) for j in range(3)]
    )

    def weights(i):
        return w_ref[i * 3 * wide : (i + 1) * 3 * wide, :]

    first = jnp.dot(
        cells, across([weights(0), weights(1)]), preferred_element_type=jnp.float32
    )
    last = jnp.dot(cells, weights(2), preferred_element_type=jnp.float32)
    rim = jnp.zeros((128, LANES), jnp.float32)
    pre = (
        jnp.concatenate([rim, first[:-128, :LANES]])
        + first[:, LANES:]
        + jnp.concatenate([last[128:], rim])
    )
    pre_ref[...] = pre.reshape(pre_ref.shape)


def against(a, b):
    return lax.dot_general(
        a, b, (((1,), (1,)), ((), ())), preferred_element_type=jnp.float32
    )


def backward_kernel(
    pre_ref,
    turned_ref,
    own_ref,
    other_ref,
    w_down_ref,
    w_up_ref,
    mine_ref,
    passed_ref,
    slab_ref,
    natural_ref,
    folded_ref,
    taps_ref,
    rows_ref,
):
    side = lax.axis_index("sp")
    core = lax.axis_index("dp") % 2
    load_crops(own_ref, other_ref, natural_ref, side)
    up = [
        natural_ref[:, :, pl.ds(parity, 8, stride=2), :].reshape(4, 2, 4, 2, 8, LANES)
        for parity in range(2)
    ]
    places = [(i, j, k) for i in range(2) for j in range(2) for k in range(2)]

    def block(i, j, k):
        return pre_ref[:, i, :, j, k].reshape(128, LANES)

    def up_block(i, j, k):
        return up[k][:, i, :, j].reshape(128, LANES)

    hidden = across([jax.nn.silu(block(*at)).astype(jnp.bfloat16) for at in places])
    upstream = across([up_block(*at).astype(jnp.bfloat16) for at in places])
    pre_deep = jnp.dot(hidden, w_down_ref[...], preferred_element_type=jnp.float32)
    deep = pre_deep.shape[1]
    grad_act = against(
        upstream, across([w_up_ref[tap * deep : (tap + 1) * deep, :] for tap in range(8)])
    )
    grad_deep = (grad_act * silu_slope(pre_deep)).astype(jnp.bfloat16)
    back = against(grad_deep, w_down_ref[...]).astype(jnp.bfloat16).astype(jnp.float32)
    for tap, at in enumerate(places):
        i, j, k = at
        summed = up_block(*at) + back[:, tap * LANES : (tap + 1) * LANES]
        folded_ref[:, i, :, j, k] = (summed * silu_slope(block(*at))).reshape(4, 4, 8, LANES)
    planes = 8
    whole = (planes, 8, 8, LANES)
    clear_rim(taps_ref, True)
    fill_taps(
        taps_ref,
        folded_ref[:, :, :, :, 0].reshape(whole),
        folded_ref[:, :, :, :, 1].reshape(whole),
    )
    slab_ref[...] = taps_ref[
        pl.ds(side * (planes // 2), planes // 2 + 2), 1:9, :, LANES : 2 * LANES
    ]

    deep_act = jax.nn.silu(pre_deep).T.astype(jnp.bfloat16)
    grad_up = jnp.dot(deep_act, upstream, preferred_element_type=jnp.float32)
    down_at = 27 * LANES
    up_at = down_at + 8 * deep
    for tap in range(8):
        rows_ref[up_at + tap * deep : up_at + (tap + 1) * deep, :] = grad_up[
            :, tap * LANES : (tap + 1) * LANES
        ]
    grad_down = jnp.dot(
        hidden.astype(jnp.float32).T.astype(jnp.bfloat16),
        grad_deep,
        preferred_element_type=jnp.float32,
    )
    for part in range(deep // LANES):
        rows_ref[pl.ds(down_at + part, 8 * LANES, stride=deep // LANES), :] = grad_down[
            :, part * LANES : (part + 1) * LANES
        ]
    turned = turned_ref[...]
    for i in range(3):
        for j in range(3):
            cells = taps_ref[i : i + planes, j : j + 8].reshape(planes * 128, 3 * LANES)
            sums = jnp.dot(turned, cells, preferred_element_type=jnp.float32)
            for k in range(3):
                at = (26 - 9 * i - 3 * j - k) * LANES
                rows_ref[at : at + LANES, :] = sums[:, k * LANES : (k + 1) * LANES]
    share = rows_ref.shape[0] // 16
    half = mine_ref.shape[1]
    for pair in range(8):
        at = 2 * pair * share + side * (share - half)
        keep = pl.multiple_of(at + core * share, 8)
        give = pl.multiple_of(at + (1 - core) * share, 8)
        mine_ref[pair] = rows_ref[pl.ds(keep, half), :].astype(jnp.bfloat16)
        passed_ref[pair] = rows_ref[pl.ds(give, half), :].astype(jnp.bfloat16)


def input_kernel(slab_ref, w_ref, out_ref, taps_ref, natural_ref):
    slab = slab_ref[...].astype(jnp.float32)
    planes = slab.shape[0]
    clear_rim(taps_ref, False)
    fill_taps(taps_ref, slab[:, :, :8], slab[:, :, 8:])
    own = planes - 2
    size = own * 128
    total = jnp.zeros((size, LANES), jnp.float32)
    for i in range(3):
        for j in range(3):
            first = 26 - 9 * i - 3 * j
            weights = across(
                [w_ref[(first - k) * LANES : (first - k + 1) * LANES, :] for k in range(3)]
            )
            cells = taps_ref[1 + i : 1 + i + own, j : j + 8].reshape(size, 3 * LANES)
            total += against(cells, weights)
    total = total.reshape(own, 8, 2, 8, LANES)
    for parity in range(2):
        natural_ref[:, :, pl.ds(parity, 8, stride=2), :] = total[:, :, parity]
    for crop in range(2):
        out_ref[crop] = natural_ref[:, :, 8 * crop : 8 * crop + 8, :].astype(jnp.bfloat16)


def kernel_call(body, outs, scratch, flops, count):
    return pl.pallas_call(
        body,
        out_shape=outs,
        in_specs=[VMEM] * count,
        out_specs=tuple(VMEM for _ in outs),
        scratch_shapes=[pltpu.VMEM(shape, kind) for shape, kind in scratch],
        compiler_params=pltpu.CompilerParams(vmem_limit_bytes=40 << 20),
        cost_estimate=pl.CostEstimate(flops=flops, bytes_accessed=1 << 21, transcendentals=0),
    )


def per_device_pairs(inputs, cotangent, w_conv, w_down, w_up):
    bf16, f32 = jnp.bfloat16, jnp.float32
    shape = jax.ShapeDtypeStruct
    other_in = swap_x(inputs)
    other_up = swap_x(cotangent)
    pre, turned = kernel_call(
        forward_kernel,
        (shape((4, 2, 4, 2, 2, 8, LANES), f32), shape((LANES, 1024), bf16)),
        [((8, 8, 16, LANES), f32), ((10, 10, 16, 3 * LANES), bf16)],
        10**9,
        3,
    )(inputs, other_in, w_conv)
    total_rows = (w_conv.size + w_down.size + w_up.size) // LANES
    per_share = total_rows // 16
    half = -(-per_share // 32) * 16
    mine, passed, slab = kernel_call(
        backward_kernel,
        (
            shape((8, half, LANES), bf16),
            shape((8, half, LANES), bf16),
            shape((6, 8, 16, LANES), bf16),
        ),
        [
            ((8, 8, 16, LANES), f32),
            ((4, 2, 4, 2, 2, 8, LANES), f32),
            ((10, 10, 16, 3 * LANES), bf16),
            ((total_rows, LANES), f32),
        ],
        10**9,
        6,
    )(pre, turned, cotangent, other_up, w_down, w_up)
    (grad_input,) = kernel_call(
        input_kernel,
        (shape(inputs.shape, bf16),),
        [((8, 10, 16, 3 * LANES), bf16), ((4, 8, 16, LANES), f32)],
        10**9,
        2,
    )(slab, w_conv)

    passed = swap_dp(passed, 1)
    crop_total = inputs.shape[0] * lax.axis_size("dp")
    scale = 1.0 / jnp.sqrt(jnp.float32(crop_total * inputs.shape[2] ** 3))
    grid = (2, 2, 2, half, LANES)
    low, high = sum_shares(mine.reshape(grid), passed.reshape(grid), scale)
    grad_share = jnp.concatenate([low, high[2 * half - per_share :]]).reshape(-1)
    return (grad_input, grad_share)


def solution(mesh):
    pairs = dict(mesh.shape) == {"sp": 2, "dp": 16}
    return jax.shard_map(
        per_device_pairs if pairs else per_device,
        mesh=mesh,
        in_specs=(P("dp", "sp", None, None, None), P("dp", "sp", None, None, None), P(), P(), P()),
        out_specs=(P("dp", "sp", None, None, None), P("dp")),
        check_vma=False,
    )
```

```python
import jax
import jax.numpy as jnp
from jax import lax
from jax.experimental import pallas as pl
from jax.experimental.pallas import tpu as pltpu
from jax.sharding import PartitionSpec as P


def extended(cells, sides, width):
    for axis, dim in sides:
        count = lax.axis_size(axis)
        ends = count - 1
        head = lax.slice_in_dim(cells, 0, width, axis=dim)
        tail = lax.slice_in_dim(cells, cells.shape[dim] - width, cells.shape[dim], axis=dim)
        cells = jnp.concatenate(
            [
                lax.ppermute(tail, axis, [(i, (i + 1) % count) for i in range(ends)]),
                cells,
                lax.ppermute(head, axis, [((i + 1) % count, i) for i in range(ends)]),
            ],
            axis=dim,
        )
    return cells


def silu_slope(pre_act):
    sigmoid_value = jax.nn.sigmoid(pre_act)
    return sigmoid_value * (1.0 + pre_act * (1.0 - sigmoid_value))


def unfold_taps(padded):
    first_size = padded.shape[1] - 2
    second_size = padded.shape[2] - 2
    third_size = padded.shape[3] - 2
    pieces = [
        padded[:, i : i + first_size, j : j + second_size, k : k + third_size, :]
        for i in range(3)
        for j in range(3)
        for k in range(3)
    ]
    stacked = jnp.concatenate(pieces, axis=-1)
    return stacked.reshape(-1, stacked.shape[-1])


def to_blocks(volume):
    shape = volume.shape
    folded = volume.reshape(
        shape[0], shape[1] // 2, 2, shape[2] // 2, 2, shape[3] // 2, 2, shape[4]
    )
    folded = folded.transpose(0, 1, 3, 5, 2, 4, 6, 7)
    return folded.reshape(-1, 8 * shape[4])


def from_blocks(blocked, shape):
    folded = blocked.reshape(
        shape[0], shape[1] // 2, shape[2] // 2, shape[3] // 2, 2, 2, 2, shape[4]
    )
    folded = folded.transpose(0, 1, 4, 2, 5, 3, 6, 7)
    return folded.reshape(shape)


def flip_taps(w_conv):
    width_in = w_conv.shape[1]
    return (
        w_conv.reshape(27, width_in, width_in)[::-1]
        .transpose(0, 2, 1)
        .reshape(27 * width_in, width_in)
    )


def deep_level(hidden, upstream, w_down, w_up):
    width_in = hidden.shape[-1]
    width_deep = w_down.shape[1]
    hid_blocks = to_blocks(hidden)
    up_blocks = to_blocks(upstream)
    pre_deep = jnp.dot(hid_blocks, w_down, preferred_element_type=jnp.float32)
    deep_act = jax.nn.silu(pre_deep).astype(jnp.bfloat16)
    w_up_back = (
        w_up.reshape(8, width_deep, width_in).transpose(0, 2, 1).reshape(8 * width_in, width_deep)
    )
    grad_act = jnp.dot(up_blocks, w_up_back, preferred_element_type=jnp.float32)
    grad_up = lax.dot_general(
        deep_act, up_blocks, (((0,), (0,)), ((), ())), preferred_element_type=jnp.float32
    )
    grad_up = (
        grad_up.reshape(width_deep, 8, width_in)
        .transpose(1, 0, 2)
        .reshape(8 * width_deep, width_in)
    )
    grad_deep = (grad_act * silu_slope(pre_deep)).astype(jnp.bfloat16)
    grad_down = lax.dot_general(
        hid_blocks, grad_deep, (((0,), (0,)), ((), ())), preferred_element_type=jnp.float32
    )
    back_blocks = jnp.dot(grad_deep, w_down.T, preferred_element_type=jnp.float32).astype(
        jnp.bfloat16
    )
    return (grad_down, grad_up, from_blocks(back_blocks, hidden.shape))


def per_device(inputs, cotangent, w_conv, w_down, w_up):
    width_in = w_conv.shape[1]
    edge_pad = ((0, 0), (0, 0), (1, 1), (1, 1), (0, 0))
    slab_in = extended(inputs, (("sp", 1),), 1)
    columns = unfold_taps(jnp.pad(slab_in, edge_pad))
    pre_conv = jnp.dot(columns, w_conv, preferred_element_type=jnp.float32)
    hidden = jax.nn.silu(pre_conv).astype(jnp.bfloat16).reshape(inputs.shape)
    hidden_crops, upstream_crops = (
        lax.all_to_all(hidden, "sp", split_axis=0, concat_axis=1, tiled=True),
        lax.all_to_all(cotangent, "sp", split_axis=0, concat_axis=1, tiled=True),
    )
    grad_down, grad_up, back_down = deep_level(hidden_crops, upstream_crops, w_down, w_up)
    back_slab = lax.all_to_all(back_down, "sp", split_axis=1, concat_axis=0, tiled=True)
    summed = cotangent.astype(jnp.float32).reshape(-1, width_in) + back_slab.astype(
        jnp.float32
    ).reshape(-1, width_in)
    grad_pre = (summed * silu_slope(pre_conv)).astype(jnp.bfloat16)
    grad_conv = lax.dot_general(
        columns, grad_pre, (((0,), (0,)), ((), ())), preferred_element_type=jnp.float32
    )
    padded_grad = extended(grad_pre.reshape(inputs.shape), (("sp", 1),), 1)
    grad_input = jnp.dot(
        unfold_taps(jnp.pad(padded_grad, edge_pad)),
        flip_taps(w_conv),
        preferred_element_type=jnp.float32,
    )
    grad_input = grad_input.astype(jnp.bfloat16).reshape(inputs.shape)
    local_sums = jnp.concatenate(
        [grad_conv.reshape(-1), grad_down.reshape(-1), grad_up.reshape(-1)]
    )
    within_group = lax.psum(local_sums.astype(jnp.bfloat16), "sp").astype(jnp.float32)
    grad_share = lax.psum_scatter(within_group, "dp", scatter_dimension=0, tiled=True)
    edge_cells = inputs.shape[2]
    crop_total = inputs.shape[0] * lax.axis_size("dp")
    norm_factor = 1.0 / jnp.sqrt(jnp.float32(crop_total * edge_cells * edge_cells * edge_cells))
    return (grad_input, grad_share * norm_factor)


def swap_x(value):
    return lax.ppermute(value, "sp", [(0, 1), (1, 0)])


def swap_dp(value, mask):
    return lax.ppermute(value, "dp", [(i, i ^ mask) for i in range(16)])


def pick(value, dim, index):
    return lax.dynamic_index_in_dim(value, index, dim, keepdims=False)


def sum_shares(mine, passed, scale):
    at = lax.axis_index("dp")
    side = lax.axis_index("sp")
    row, near, far = (at >> 1) & 1, (at >> 2) & 1, (at >> 3) & 1

    def chip_sum(z, y):
        return pick(pick(mine, 1, z), 1, y).astype(jnp.float32) + pick(
            pick(passed, 1, z), 1, y
        ).astype(jnp.float32)

    diagonal = swap_dp(chip_sum(1 - near, 1 - row).astype(jnp.bfloat16), 6)
    along_y = swap_dp(chip_sum(near, 1 - row).astype(jnp.bfloat16), 2)
    along_z = swap_dp(chip_sum(1 - near, row).astype(jnp.bfloat16), 4)
    square = (
        chip_sum(near, row)
        + along_y.astype(jnp.float32)
        + along_z.astype(jnp.float32)
        + diagonal.astype(jnp.float32)
    )
    across = swap_dp(pick(square, 0, 1 - far).astype(jnp.bfloat16), 8)
    total = (pick(square, 0, far) + across.astype(jnp.float32)).astype(jnp.bfloat16)
    other = swap_x(total)
    low = jnp.where(side == 0, total, other)
    high = jnp.where(side == 0, other, total)
    return low.astype(jnp.float32) * scale, high.astype(jnp.float32) * scale


LANES = 128
VMEM = pl.BlockSpec(memory_space=pltpu.VMEM)
BF16, F32 = jnp.bfloat16, jnp.float32
PLACES = tuple((i, j, k) for i in range(2) for j in range(2) for k in range(2))


def dot(a, b):
    return jnp.dot(a, b, preferred_element_type=F32)


def against(a, b):
    return lax.dot_general(a, b, (((1,), (1,)), ((), ())), preferred_element_type=F32)


def across(parts):
    return jnp.concatenate(parts, axis=-1)


def split_parity(slab_ref, natural_ref):
    for crop in range(2):
        natural_ref[:, :, 8 * crop : 8 * crop + 8, :] = slab_ref[crop].astype(F32)
    return [natural_ref[:, :, pl.ds(parity, 8, stride=2), :] for parity in range(2)]


def fill_taps(taps_ref, even, odd):
    planes = even.shape[0]
    kk = lax.broadcasted_iota(jnp.int32, even.shape, 2) % 4
    before = jnp.where(kk == 0, 0.0, pltpu.roll(odd, 1, 2))
    after = jnp.where(kk == 3, 0.0, pltpu.roll(even, 7, 2))
    for tap, (low, high) in enumerate(((before, even), (even, odd), (odd, after))):
        taps_ref[1 : 1 + planes, pl.ds(1, 8), :, tap * LANES : (tap + 1) * LANES] = jnp.concatenate(
            [low, high], axis=2
        ).astype(BF16)


def clear_rim(taps_ref, with_planes):
    planes, rows, tile, lanes = taps_ref.shape
    row = jnp.zeros((planes, tile, lanes), BF16)
    taps_ref[:, 0] = row
    taps_ref[:, rows - 1] = row
    if with_planes:
        plane = jnp.zeros((rows, tile, lanes), BF16)
        taps_ref[0] = plane
        taps_ref[planes - 1] = plane


def slab_conv(slab_ref, w_ref, natural_ref, taps_ref):
    even, odd = split_parity(slab_ref, natural_ref)
    clear_rim(taps_ref, False)
    fill_taps(taps_ref, even, odd)
    planes = even.shape[0]
    size = planes * 128
    wide = 3 * LANES
    centre = taps_ref[1 : 1 + planes, 1:9, :, LANES : 2 * LANES].reshape(size, LANES)
    turned = centre.astype(F32).T.astype(BF16)
    cells = across([taps_ref[1 : 1 + planes, j : j + 8].reshape(size, wide) for j in range(3)])

    def weights(i):
        return w_ref[i * 3 * wide : (i + 1) * 3 * wide, :]

    first = dot(cells, across([weights(0), weights(1)])).reshape(planes, 128, 2 * LANES)
    last = dot(cells, weights(2)).reshape(planes, 128, LANES)
    none = jnp.zeros((1, 128, LANES), F32)
    two = jnp.zeros((2, 128, LANES), F32)
    added = (
        jnp.concatenate([two, first[:, :, :LANES]])
        + jnp.concatenate([none, first[:, :, LANES:], none])
        + jnp.concatenate([last, two])
    )
    return added, turned


def blocks(parts, tap):
    i, j, k = PLACES[tap]
    even_odd = parts[k]
    planes = even_odd.shape[0]
    folded = even_odd.reshape(planes // 2, 2, 4, 2, 8, LANES)
    return folded[:, i, :, j].reshape(planes * 16, LANES)


def deep_gradient(parts, w_up_ref):
    upstream = across([blocks(parts, tap).astype(BF16) for tap in range(8)])
    deep = w_up_ref.shape[0] // 8
    w_up = across([w_up_ref[tap * deep : (tap + 1) * deep, :] for tap in range(8)])
    return upstream, against(upstream, w_up)


def own_kernel(in_ref, w_ref, add_ref, turned_ref, natural_ref, taps_ref):
    add_ref[...], turned_ref[...] = slab_conv(in_ref, w_ref, natural_ref, taps_ref)


def forward_kernel(
    in_ref,
    w_ref,
    add_ref,
    turned_own_ref,
    w_down_ref,
    up_ref,
    w_up_ref,
    slope_ref,
    turned_ref,
    hidden_ref,
    act_ref,
    deep_slope_ref,
    blocks_own_ref,
    act_own_ref,
    natural_ref,
    taps_ref,
    sum_ref,
):
    side = lax.axis_index("sp")
    planes = in_ref.shape[1]
    added, turned = slab_conv(in_ref, w_ref, natural_ref, taps_ref)
    sum_ref[...] = jnp.zeros_like(sum_ref)
    sum_ref[pl.ds(side * planes, planes + 2)] = add_ref[...]
    sum_ref[pl.ds((1 - side) * planes, planes + 2)] += added
    turned_ref[side] = turned_own_ref[...]
    turned_ref[1 - side] = turned
    folded = (planes, 2, 4, 2, 2, 8, LANES)
    pre = sum_ref[1 : 1 + 2 * planes].reshape(folded)
    sigmoid_value = jax.nn.sigmoid(pre)
    slope_ref[...] = sigmoid_value * (1.0 + pre * (1.0 - sigmoid_value))
    act = pre * sigmoid_value
    hidden = across([act[:, i, :, j, k].reshape(128, LANES).astype(BF16) for i, j, k in PLACES])
    hidden_ref[...] = hidden.astype(F32).T.astype(BF16)
    pre_deep = dot(hidden, w_down_ref[...])
    act_ref[...] = jax.nn.silu(pre_deep).T.astype(BF16)
    deep_slope_ref[...] = silu_slope(pre_deep)
    blocks_own_ref[...], act_own_ref[...] = deep_gradient(
        split_parity(up_ref, natural_ref), w_up_ref
    )


def backward_kernel(
    up_ref,
    slope_ref,
    turned_ref,
    hidden_ref,
    deep_act_ref,
    deep_slope_ref,
    blocks_own_ref,
    act_own_ref,
    w_down_ref,
    w_up_ref,
    mine_ref,
    passed_ref,
    slab_ref,
    natural_ref,
    blocks_ref,
    act_ref,
    folded_ref,
    taps_ref,
    rows_ref,
):
    side = lax.axis_index("sp")
    core = lax.axis_index("dp") % 2
    parts = split_parity(up_ref, natural_ref)
    upstream, grad_act = deep_gradient(parts, w_up_ref)
    blocks_ref[side] = blocks_own_ref[...]
    blocks_ref[1 - side] = upstream
    act_ref[side] = act_own_ref[...]
    act_ref[1 - side] = grad_act
    upstream = blocks_ref[...].reshape(128, 8 * LANES)
    grad_deep = (act_ref[...].reshape(deep_slope_ref.shape) * deep_slope_ref[...]).astype(BF16)
    back = against(grad_deep, w_down_ref[...]).astype(BF16).astype(F32)
    for tap, (i, j, k) in enumerate(PLACES):
        lanes = slice(tap * LANES, (tap + 1) * LANES)
        summed = (upstream[:, lanes].astype(F32) + back[:, lanes]).reshape(4, 4, 8, LANES)
        folded_ref[:, i, :, j, k] = summed * slope_ref[:, i, :, j, k]
    planes = 8
    whole = (planes, 8, 8, LANES)
    clear_rim(taps_ref, True)
    fill_taps(
        taps_ref,
        folded_ref[:, :, :, :, 0].reshape(whole),
        folded_ref[:, :, :, :, 1].reshape(whole),
    )
    slab_ref[...] = taps_ref[
        pl.ds(side * (planes // 2), planes // 2 + 2), 1:9, :, LANES : 2 * LANES
    ]

    deep = w_down_ref.shape[1]
    grad_up = dot(deep_act_ref[...], upstream)
    down_at = 27 * LANES
    up_at = down_at + 8 * deep
    for tap in range(8):
        rows_ref[up_at + tap * deep : up_at + (tap + 1) * deep, :] = grad_up[
            :, tap * LANES : (tap + 1) * LANES
        ]
    grad_down = dot(hidden_ref[...], grad_deep)
    for part in range(deep // LANES):
        rows_ref[pl.ds(down_at + part, 8 * LANES, stride=deep // LANES), :] = grad_down[
            :, part * LANES : (part + 1) * LANES
        ]
    turned = across([turned_ref[0], turned_ref[1]])
    for i in range(3):
        cells = across(
            [
                taps_ref[i : i + planes, j : j + 8].reshape(planes * 128, 3 * LANES)
                for j in range(3)
            ]
        )
        sums = dot(turned, cells)
        for tap in range(9):
            at = (26 - 9 * i - tap) * LANES
            rows_ref[at : at + LANES, :] = sums[:, tap * LANES : (tap + 1) * LANES]
    share = rows_ref.shape[0] // 16
    half = mine_ref.shape[1]
    for pair in range(8):
        at = 2 * pair * share + side * (share - half)
        keep = pl.multiple_of(at + core * share, 8)
        give = pl.multiple_of(at + (1 - core) * share, 8)
        mine_ref[pair] = rows_ref[pl.ds(keep, half), :].astype(BF16)
        passed_ref[pair] = rows_ref[pl.ds(give, half), :].astype(BF16)


def input_kernel(slab_ref, w_ref, out_ref, taps_ref, natural_ref):
    slab = slab_ref[...].astype(F32)
    own = slab.shape[0] - 2
    size = own * 128
    clear_rim(taps_ref, False)
    fill_taps(taps_ref, slab[:, :, :8], slab[:, :, 8:])
    total = jnp.zeros((size, LANES), F32)
    for i in range(3):
        for j in range(3):
            first = 26 - 9 * i - 3 * j
            weights = across(
                [w_ref[(first - k) * LANES : (first - k + 1) * LANES, :] for k in range(3)]
            )
            cells = taps_ref[1 + i : 1 + i + own, j : j + 8].reshape(size, 3 * LANES)
            total += against(cells, weights)
    total = total.reshape(own, 8, 2, 8, LANES)
    for parity in range(2):
        natural_ref[:, :, pl.ds(parity, 8, stride=2), :] = total[:, :, parity]
    for crop in range(2):
        out_ref[crop] = natural_ref[:, :, 8 * crop : 8 * crop + 8, :].astype(BF16)


def run(body, operands, outs, scratch, flops):
    return pl.pallas_call(
        body,
        out_shape=tuple(jax.ShapeDtypeStruct(shape, kind) for shape, kind in outs),
        in_specs=[VMEM] * len(operands),
        out_specs=(VMEM,) * len(outs),
        scratch_shapes=[pltpu.VMEM(shape, kind) for shape, kind in scratch],
        compiler_params=pltpu.CompilerParams(vmem_limit_bytes=40 << 20),
        cost_estimate=pl.CostEstimate(flops=flops, bytes_accessed=1 << 21, transcendentals=0),
    )(*operands)


def per_device_pairs(inputs, cotangent, w_conv, w_down, w_up):
    deep = w_down.shape[1]
    other_in = swap_x(inputs)
    other_up = swap_x(cotangent)
    natural = ((4, 8, 16, LANES), F32)
    slab_taps = ((6, 10, 16, 3 * LANES), BF16)
    blocked = ((64, 8 * LANES), BF16)
    act = ((64, deep), F32)
    added, turned_own = run(
        own_kernel,
        (inputs, w_conv),
        [((6, 128, LANES), F32), ((LANES, 512), BF16)],
        [natural, slab_taps],
        10**9,
    )
    folded = ((4, 2, 4, 2, 2, 8, LANES), F32)
    saved = run(
        forward_kernel,
        (other_in, w_conv, added, turned_own, w_down, cotangent, w_up),
        [
            folded,
            ((2, LANES, 512), BF16),
            ((8 * LANES, 128), BF16),
            ((deep, 128), BF16),
            ((128, deep), F32),
            blocked,
            act,
        ],
        [natural, slab_taps, ((10, 128, LANES), F32)],
        10**9,
    )
    total_rows = (w_conv.size + w_down.size + w_up.size) // LANES
    per_share = total_rows // 16
    half = -(-per_share // 32) * 16
    mine, passed, slab = run(
        backward_kernel,
        (other_up, *saved, w_down, w_up),
        [((8, half, LANES), BF16), ((8, half, LANES), BF16), ((6, 8, 16, LANES), BF16)],
        [
            natural,
            ((2, *blocked[0]), BF16),
            ((2, *act[0]), F32),
            folded,
            ((10, 10, 16, 3 * LANES), BF16),
            ((total_rows, LANES), F32),
        ],
        10**9,
    )
    (grad_input,) = run(
        input_kernel,
        (slab, w_conv),
        [(inputs.shape, BF16)],
        [((8, 10, 16, 3 * LANES), BF16), natural],
        10**9,
    )

    passed = swap_dp(passed, 1)
    crop_total = inputs.shape[0] * lax.axis_size("dp")
    scale = 1.0 / jnp.sqrt(jnp.float32(crop_total * inputs.shape[2] ** 3))
    grid = (2, 2, 2, half, LANES)
    low, high = sum_shares(mine.reshape(grid), passed.reshape(grid), scale)
    grad_share = jnp.concatenate([low, high[2 * half - per_share :]]).reshape(-1)
    return (grad_input, grad_share)


def solution(mesh):
    pairs = dict(mesh.shape) == {"sp": 2, "dp": 16}
    return jax.shard_map(
        per_device_pairs if pairs else per_device,
        mesh=mesh,
        in_specs=(P("dp", "sp", None, None, None), P("dp", "sp", None, None, None), P(), P(), P()),
        out_specs=(P("dp", "sp", None, None, None), P("dp")),
        check_vma=False,
    )
```

```python
import functools

import jax
import jax.numpy as jnp
from jax import lax
from jax.experimental import pallas as pl
from jax.experimental.pallas import tpu as pltpu
from jax.sharding import PartitionSpec as P


def extended(cells, sides, width):
    for axis, dim in sides:
        count = lax.axis_size(axis)
        ends = count - 1
        head = lax.slice_in_dim(cells, 0, width, axis=dim)
        tail = lax.slice_in_dim(cells, cells.shape[dim] - width, cells.shape[dim], axis=dim)
        cells = jnp.concatenate(
            [
                lax.ppermute(tail, axis, [(i, (i + 1) % count) for i in range(ends)]),
                cells,
                lax.ppermute(head, axis, [((i + 1) % count, i) for i in range(ends)]),
            ],
            axis=dim,
        )
    return cells


def silu_slope(pre_act):
    sigmoid_value = jax.nn.sigmoid(pre_act)
    return sigmoid_value * (1.0 + pre_act * (1.0 - sigmoid_value))


def unfold_taps(padded):
    first_size = padded.shape[1] - 2
    second_size = padded.shape[2] - 2
    third_size = padded.shape[3] - 2
    pieces = [
        padded[:, i : i + first_size, j : j + second_size, k : k + third_size, :]
        for i in range(3)
        for j in range(3)
        for k in range(3)
    ]
    stacked = jnp.concatenate(pieces, axis=-1)
    return stacked.reshape(-1, stacked.shape[-1])


def to_blocks(volume):
    shape = volume.shape
    folded = volume.reshape(
        shape[0], shape[1] // 2, 2, shape[2] // 2, 2, shape[3] // 2, 2, shape[4]
    )
    folded = folded.transpose(0, 1, 3, 5, 2, 4, 6, 7)
    return folded.reshape(-1, 8 * shape[4])


def from_blocks(blocked, shape):
    folded = blocked.reshape(
        shape[0], shape[1] // 2, shape[2] // 2, shape[3] // 2, 2, 2, 2, shape[4]
    )
    folded = folded.transpose(0, 1, 4, 2, 5, 3, 6, 7)
    return folded.reshape(shape)


def flip_taps(w_conv):
    width_in = w_conv.shape[1]
    return (
        w_conv.reshape(27, width_in, width_in)[::-1]
        .transpose(0, 2, 1)
        .reshape(27 * width_in, width_in)
    )


def deep_level(hidden, upstream, w_down, w_up):
    width_in = hidden.shape[-1]
    width_deep = w_down.shape[1]
    hid_blocks = to_blocks(hidden)
    up_blocks = to_blocks(upstream)
    pre_deep = jnp.dot(hid_blocks, w_down, preferred_element_type=jnp.float32)
    deep_act = jax.nn.silu(pre_deep).astype(jnp.bfloat16)
    w_up_back = (
        w_up.reshape(8, width_deep, width_in).transpose(0, 2, 1).reshape(8 * width_in, width_deep)
    )
    grad_act = jnp.dot(up_blocks, w_up_back, preferred_element_type=jnp.float32)
    grad_up = lax.dot_general(
        deep_act, up_blocks, (((0,), (0,)), ((), ())), preferred_element_type=jnp.float32
    )
    grad_up = (
        grad_up.reshape(width_deep, 8, width_in)
        .transpose(1, 0, 2)
        .reshape(8 * width_deep, width_in)
    )
    grad_deep = (grad_act * silu_slope(pre_deep)).astype(jnp.bfloat16)
    grad_down = lax.dot_general(
        hid_blocks, grad_deep, (((0,), (0,)), ((), ())), preferred_element_type=jnp.float32
    )
    back_blocks = jnp.dot(grad_deep, w_down.T, preferred_element_type=jnp.float32).astype(
        jnp.bfloat16
    )
    return (grad_down, grad_up, from_blocks(back_blocks, hidden.shape))


def per_device(inputs, cotangent, w_conv, w_down, w_up):
    width_in = w_conv.shape[1]
    edge_pad = ((0, 0), (0, 0), (1, 1), (1, 1), (0, 0))
    slab_in = extended(inputs, (("sp", 1),), 1)
    columns = unfold_taps(jnp.pad(slab_in, edge_pad))
    pre_conv = jnp.dot(columns, w_conv, preferred_element_type=jnp.float32)
    hidden = jax.nn.silu(pre_conv).astype(jnp.bfloat16).reshape(inputs.shape)
    hidden_crops, upstream_crops = (
        lax.all_to_all(hidden, "sp", split_axis=0, concat_axis=1, tiled=True),
        lax.all_to_all(cotangent, "sp", split_axis=0, concat_axis=1, tiled=True),
    )
    grad_down, grad_up, back_down = deep_level(hidden_crops, upstream_crops, w_down, w_up)
    back_slab = lax.all_to_all(back_down, "sp", split_axis=1, concat_axis=0, tiled=True)
    summed = cotangent.astype(jnp.float32).reshape(-1, width_in) + back_slab.astype(
        jnp.float32
    ).reshape(-1, width_in)
    grad_pre = (summed * silu_slope(pre_conv)).astype(jnp.bfloat16)
    grad_conv = lax.dot_general(
        columns, grad_pre, (((0,), (0,)), ((), ())), preferred_element_type=jnp.float32
    )
    padded_grad = extended(grad_pre.reshape(inputs.shape), (("sp", 1),), 1)
    grad_input = jnp.dot(
        unfold_taps(jnp.pad(padded_grad, edge_pad)),
        flip_taps(w_conv),
        preferred_element_type=jnp.float32,
    )
    grad_input = grad_input.astype(jnp.bfloat16).reshape(inputs.shape)
    local_sums = jnp.concatenate(
        [grad_conv.reshape(-1), grad_down.reshape(-1), grad_up.reshape(-1)]
    )
    within_group = lax.psum(local_sums.astype(jnp.bfloat16), "sp").astype(jnp.float32)
    grad_share = lax.psum_scatter(within_group, "dp", scatter_dimension=0, tiled=True)
    edge_cells = inputs.shape[2]
    crop_total = inputs.shape[0] * lax.axis_size("dp")
    norm_factor = 1.0 / jnp.sqrt(jnp.float32(crop_total * edge_cells * edge_cells * edge_cells))
    return (grad_input, grad_share * norm_factor)


def swap_x(value):
    return lax.ppermute(value, "sp", [(0, 1), (1, 0)])


def swap_dp(value, mask, odd_mask=None):
    masks = (mask, mask if odd_mask is None else odd_mask)
    return lax.ppermute(value, "dp", [(i, i ^ masks[i % 2]) for i in range(16)])


def pick(value, dim, index):
    return lax.dynamic_index_in_dim(value, index, dim, keepdims=False)


def square_sum(mine, passed):
    here = (lax.axis_index("dp") >> 1) & 3

    def chip_sum(index):
        return pick(mine, 1, index).astype(jnp.float32) + pick(passed, 1, index).astype(
            jnp.float32
        )

    core = lax.axis_index("dp") & 1
    received = [
        swap_dp(chip_sum(here ^ jnp.where(core == 0, even, odd)).astype(jnp.bfloat16), 2 * even, 2 * odd)
        for even, odd in ((1, 3), (2, 1), (3, 2))
    ]
    total = chip_sum(here)
    for part in received:
        total += part.astype(jnp.float32)
    return total


def end_sum(square, scale, pieces):
    far = (lax.axis_index("dp") >> 3) & 1
    side = lax.axis_index("sp")
    sent = pick(square, 0, 1 - far).astype(jnp.bfloat16)
    kept = pick(square, 0, far)
    lows, highs = [], []
    received = [swap_dp(sent[first:last], 8) for first, last in pieces]
    for (first, last), part in zip(pieces, received):
        total = (kept[first:last] + part.astype(jnp.float32)).astype(jnp.bfloat16)
        other = swap_x(total)
        lows.append(jnp.where(side == 0, total, other).astype(jnp.float32) * scale)
        highs.append(jnp.where(side == 0, other, total).astype(jnp.float32) * scale)
    return lows, highs


LANES = 128
VMEM = pl.BlockSpec(memory_space=pltpu.VMEM)
BF16, F32 = jnp.bfloat16, jnp.float32
CHUNK = 10
PLACES = tuple((i, j, k) for i in range(2) for j in range(2) for k in range(2))


def dot(a, b):
    return jnp.dot(a, b, preferred_element_type=F32)


def against(a, b):
    return lax.dot_general(a, b, (((1,), (1,)), ((), ())), preferred_element_type=F32)


def across(parts):
    return jnp.concatenate(parts, axis=-1)


def split_parity(slab_ref, natural_ref):
    for crop in range(2):
        natural_ref[:, :, 8 * crop : 8 * crop + 8, :] = slab_ref[crop].astype(F32)
    return [natural_ref[:, :, pl.ds(parity, 8, stride=2), :] for parity in range(2)]


def fill_taps(taps_ref, even, odd):
    planes = even.shape[0]
    kk = lax.broadcasted_iota(jnp.int32, even.shape, 2) % 4
    before = jnp.where(kk == 0, 0.0, pltpu.roll(odd, 1, 2))
    after = jnp.where(kk == 3, 0.0, pltpu.roll(even, 7, 2))
    for tap, (low, high) in enumerate(((before, even), (even, odd), (odd, after))):
        taps_ref[1 : 1 + planes, pl.ds(1, 8), :, tap * LANES : (tap + 1) * LANES] = jnp.concatenate(
            [low, high], axis=2
        ).astype(BF16)


def clear_rim(taps_ref, with_planes):
    planes, rows, tile, lanes = taps_ref.shape
    row = jnp.zeros((planes, tile, lanes), BF16)
    taps_ref[:, 0] = row
    taps_ref[:, rows - 1] = row
    if with_planes:
        plane = jnp.zeros((rows, tile, lanes), BF16)
        taps_ref[0] = plane
        taps_ref[planes - 1] = plane


def slab_conv(slab_ref, w_ref, natural_ref, taps_ref):
    even, odd = split_parity(slab_ref, natural_ref)
    clear_rim(taps_ref, False)
    fill_taps(taps_ref, even, odd)
    planes = even.shape[0]
    size = planes * 128
    wide = 3 * LANES
    centre = taps_ref[1 : 1 + planes, 1:9, :, LANES : 2 * LANES].reshape(size, LANES)
    turned = centre.astype(F32).T.astype(BF16)
    cells = across([taps_ref[1 : 1 + planes, j : j + 8].reshape(size, wide) for j in range(3)])

    def weights(i):
        return w_ref[i * 3 * wide : (i + 1) * 3 * wide, :]

    first = dot(cells, across([weights(0), weights(1)])).reshape(planes, 128, 2 * LANES)
    last = dot(cells, weights(2)).reshape(planes, 128, LANES)
    none = jnp.zeros((1, 128, LANES), F32)
    two = jnp.zeros((2, 128, LANES), F32)
    added = (
        jnp.concatenate([two, first[:, :, :LANES]])
        + jnp.concatenate([none, first[:, :, LANES:], none])
        + jnp.concatenate([last, two])
    )
    return added, turned


def blocks(parts, tap):
    i, j, k = PLACES[tap]
    even_odd = parts[k]
    planes = even_odd.shape[0]
    folded = even_odd.reshape(planes // 2, 2, 4, 2, 8, LANES)
    return folded[:, i, :, j].reshape(planes * 16, LANES)


def deep_gradient(parts, w_up_ref):
    upstream = across([blocks(parts, tap).astype(BF16) for tap in range(8)])
    deep = w_up_ref.shape[0] // 8
    w_up = across([w_up_ref[tap * deep : (tap + 1) * deep, :] for tap in range(8)])
    return upstream, against(upstream, w_up)


def own_kernel(in_ref, w_ref, add_ref, turned_ref, natural_ref, taps_ref):
    add_ref[...], turned_ref[...] = slab_conv(in_ref, w_ref, natural_ref, taps_ref)


def forward_kernel(
    in_ref,
    w_ref,
    add_ref,
    turned_own_ref,
    w_down_ref,
    up_ref,
    w_up_ref,
    slope_ref,
    turned_ref,
    hidden_ref,
    act_ref,
    deep_slope_ref,
    blocks_own_ref,
    act_own_ref,
    natural_ref,
    taps_ref,
    sum_ref,
):
    side = lax.axis_index("sp")
    planes = in_ref.shape[1]
    added, turned = slab_conv(in_ref, w_ref, natural_ref, taps_ref)
    sum_ref[...] = jnp.zeros_like(sum_ref)
    sum_ref[pl.ds(side * planes, planes + 2)] = add_ref[...]
    sum_ref[pl.ds((1 - side) * planes, planes + 2)] += added
    turned_ref[side] = turned_own_ref[...]
    turned_ref[1 - side] = turned
    folded = (planes, 2, 4, 2, 2, 8, LANES)
    pre = sum_ref[1 : 1 + 2 * planes].reshape(folded)
    sigmoid_value = jax.nn.sigmoid(pre)
    slope_ref[...] = sigmoid_value * (1.0 + pre * (1.0 - sigmoid_value))
    act = pre * sigmoid_value
    hidden = across([act[:, i, :, j, k].reshape(128, LANES).astype(BF16) for i, j, k in PLACES])
    hidden_ref[...] = hidden.astype(F32).T.astype(BF16)
    pre_deep = dot(hidden, w_down_ref[...])
    act_ref[...] = jax.nn.silu(pre_deep).T.astype(BF16)
    deep_slope_ref[...] = silu_slope(pre_deep)
    blocks_own_ref[...], act_own_ref[...] = deep_gradient(
        split_parity(up_ref, natural_ref), w_up_ref
    )


def backward_kernel(
    up_ref,
    slope_ref,
    turned_ref,
    hidden_ref,
    deep_act_ref,
    deep_slope_ref,
    blocks_own_ref,
    act_own_ref,
    w_down_ref,
    w_up_ref,
    mine_ref,
    passed_ref,
    slab_ref,
    natural_ref,
    blocks_ref,
    act_ref,
    folded_ref,
    taps_ref,
    rows_ref,
):
    side = lax.axis_index("sp")
    core = lax.axis_index("dp") % 2
    parts = split_parity(up_ref, natural_ref)
    upstream, grad_act = deep_gradient(parts, w_up_ref)
    blocks_ref[side] = blocks_own_ref[...]
    blocks_ref[1 - side] = upstream
    act_ref[side] = act_own_ref[...]
    act_ref[1 - side] = grad_act
    upstream = blocks_ref[...].reshape(128, 8 * LANES)
    grad_deep = (act_ref[...].reshape(deep_slope_ref.shape) * deep_slope_ref[...]).astype(BF16)
    back = against(grad_deep, w_down_ref[...]).astype(BF16).astype(F32)
    for tap, (i, j, k) in enumerate(PLACES):
        lanes = slice(tap * LANES, (tap + 1) * LANES)
        summed = (upstream[:, lanes].astype(F32) + back[:, lanes]).reshape(4, 4, 8, LANES)
        folded_ref[:, i, :, j, k] = summed * slope_ref[:, i, :, j, k]
    planes = 8
    whole = (planes, 8, 8, LANES)
    clear_rim(taps_ref, True)
    fill_taps(
        taps_ref,
        folded_ref[:, :, :, :, 0].reshape(whole),
        folded_ref[:, :, :, :, 1].reshape(whole),
    )
    slab_ref[...] = taps_ref[
        pl.ds(side * (planes // 2), planes // 2 + 2), 1:9, :, LANES : 2 * LANES
    ]

    deep = deep_act_ref.shape[0]
    grad_up = dot(deep_act_ref[...], upstream)
    down_at = 27 * LANES
    up_at = down_at + 8 * deep
    for tap in range(8):
        rows_ref[up_at + tap * deep : up_at + (tap + 1) * deep, :] = grad_up[
            :, tap * LANES : (tap + 1) * LANES
        ]
    grad_down = dot(hidden_ref[...], grad_deep)
    for part in range(deep // LANES):
        rows_ref[pl.ds(down_at + part, 8 * LANES, stride=deep // LANES), :] = grad_down[
            :, part * LANES : (part + 1) * LANES
        ]
    for half in range(2):
        pl.when(side == half)(
            functools.partial(
                weight_rows,
                half,
                core,
                turned_ref,
                taps_ref,
                rows_ref,
                mine_ref,
                passed_ref,
            )
        )


def weight_rows(side, core, turned_ref, taps_ref, rows_ref, mine_ref, passed_ref):
    share = rows_ref.shape[0] // 16
    half = mine_ref.shape[1]
    starts = [at * share + side * (share - half) for at in range(16)]
    kept = [
        tap
        for tap in range(27)
        if any(at < (tap + 1) * LANES and tap * LANES < at + half for at in starts)
    ]
    turned = across([turned_ref[0], turned_ref[1]])
    planes = taps_ref.shape[0] - 2
    size = planes * 128
    for first in range(0, len(kept), CHUNK):
        group = kept[first : first + CHUNK]
        cells = []
        for tap in group:
            i, j, k = (26 - tap) // 9, (26 - tap) // 3 % 3, (26 - tap) % 3
            cells.append(
                taps_ref[i : i + planes, j : j + 8, :, k * LANES : (k + 1) * LANES].reshape(
                    size, LANES
                )
            )
        sums = dot(turned, across(cells))
        for at, tap in enumerate(group):
            rows_ref[tap * LANES : (tap + 1) * LANES, :] = sums[:, at * LANES : (at + 1) * LANES]
    for pair in range(8):
        for target, owner in ((mine_ref, core), (passed_ref, 1 - core)):
            rows = pl.ds(pl.multiple_of(starts[2 * pair] + owner * share, 8), half)
            target[pair] = rows_ref[rows, :].astype(BF16)


def input_kernel(slab_ref, w_ref, out_ref, taps_ref, natural_ref):
    slab = slab_ref[...].astype(F32)
    own = slab.shape[0] - 2
    size = own * 128
    clear_rim(taps_ref, False)
    fill_taps(taps_ref, slab[:, :, :8], slab[:, :, 8:])
    total = jnp.zeros((size, LANES), F32)
    for i in range(3):
        for j in range(3):
            first = 26 - 9 * i - 3 * j
            weights = across(
                [w_ref[(first - k) * LANES : (first - k + 1) * LANES, :] for k in range(3)]
            )
            cells = taps_ref[1 + i : 1 + i + own, j : j + 8].reshape(size, 3 * LANES)
            total += against(cells, weights)
    total = total.reshape(own, 8, 2, 8, LANES)
    for parity in range(2):
        natural_ref[:, :, pl.ds(parity, 8, stride=2), :] = total[:, :, parity]
    for crop in range(2):
        out_ref[crop] = natural_ref[:, :, 8 * crop : 8 * crop + 8, :].astype(BF16)


def run(body, operands, outs, scratch, flops):
    return pl.pallas_call(
        body,
        out_shape=tuple(jax.ShapeDtypeStruct(shape, kind) for shape, kind in outs),
        in_specs=[VMEM] * len(operands),
        out_specs=(VMEM,) * len(outs),
        scratch_shapes=[pltpu.VMEM(shape, kind) for shape, kind in scratch],
        compiler_params=pltpu.CompilerParams(vmem_limit_bytes=40 << 20),
        cost_estimate=pl.CostEstimate(flops=flops, bytes_accessed=1 << 21, transcendentals=0),
    )(*operands)


def per_device_pairs(inputs, cotangent, w_conv, w_down, w_up):
    deep = w_down.shape[1]
    other_in = swap_x(inputs)
    other_up = swap_x(cotangent)
    natural = ((4, 8, 16, LANES), F32)
    slab_taps = ((6, 10, 16, 3 * LANES), BF16)
    blocked = ((64, 8 * LANES), BF16)
    act = ((64, deep), F32)
    added, turned_own = run(
        own_kernel,
        (inputs, w_conv),
        [((6, 128, LANES), F32), ((LANES, 512), BF16)],
        [natural, slab_taps],
        10**9,
    )
    folded = ((4, 2, 4, 2, 2, 8, LANES), F32)
    saved = run(
        forward_kernel,
        (other_in, w_conv, added, turned_own, w_down, cotangent, w_up),
        [
            folded,
            ((2, LANES, 512), BF16),
            ((8 * LANES, 128), BF16),
            ((deep, 128), BF16),
            ((128, deep), F32),
            blocked,
            act,
        ],
        [natural, slab_taps, ((10, 128, LANES), F32)],
        10**9,
    )
    total_rows = (w_conv.size + w_down.size + w_up.size) // LANES
    per_share = total_rows // 16
    half = -(-per_share // 32) * 16
    mine, passed, slab = run(
        backward_kernel,
        (other_up, *saved, w_down, w_up),
        [((8, half, LANES), BF16), ((8, half, LANES), BF16), ((6, 8, 16, LANES), BF16)],
        [
            natural,
            ((2, *blocked[0]), BF16),
            ((2, *act[0]), F32),
            folded,
            ((10, 10, 16, 3 * LANES), BF16),
            ((total_rows, LANES), F32),
        ],
        10**9,
    )
    (grad_input,) = run(
        input_kernel,
        (slab, w_conv),
        [(inputs.shape, BF16)],
        [((8, 10, 16, 3 * LANES), BF16), natural],
        10**9,
    )

    grid = (2, 4, half, LANES)
    square = square_sum(mine.reshape(grid), swap_dp(passed, 1).reshape(grid))
    crop_total = inputs.shape[0] * lax.axis_size("dp")
    scale = 1.0 / jnp.sqrt(jnp.float32(crop_total * inputs.shape[2] ** 3))
    lows, highs = end_sum(square, scale, ((0, half),))
    highs[0] = highs[0][2 * half - per_share :]
    grad_share = jnp.concatenate(lows + highs).reshape(-1)
    return (grad_input, grad_share)


def solution(mesh):
    pairs = dict(mesh.shape) == {"sp": 2, "dp": 16}
    return jax.shard_map(
        per_device_pairs if pairs else per_device,
        mesh=mesh,
        in_specs=(P("dp", "sp", None, None, None), P("dp", "sp", None, None, None), P(), P(), P()),
        out_specs=(P("dp", "sp", None, None, None), P("dp")),
        check_vma=False,
    )
```

```python
import functools

import jax
import jax.numpy as jnp
from jax import lax
from jax.experimental import pallas as pl
from jax.experimental.pallas import tpu as pltpu
from jax.sharding import PartitionSpec as P


def extended(cells, sides, width):
    for axis, dim in sides:
        count = lax.axis_size(axis)
        ends = count - 1
        head = lax.slice_in_dim(cells, 0, width, axis=dim)
        tail = lax.slice_in_dim(cells, cells.shape[dim] - width, cells.shape[dim], axis=dim)
        cells = jnp.concatenate(
            [
                lax.ppermute(tail, axis, [(i, (i + 1) % count) for i in range(ends)]),
                cells,
                lax.ppermute(head, axis, [((i + 1) % count, i) for i in range(ends)]),
            ],
            axis=dim,
        )
    return cells


def silu_slope(pre_act):
    sigmoid_value = jax.nn.sigmoid(pre_act)
    return sigmoid_value * (1.0 + pre_act * (1.0 - sigmoid_value))


def unfold_taps(padded):
    first_size = padded.shape[1] - 2
    second_size = padded.shape[2] - 2
    third_size = padded.shape[3] - 2
    pieces = [
        padded[:, i : i + first_size, j : j + second_size, k : k + third_size, :]
        for i in range(3)
        for j in range(3)
        for k in range(3)
    ]
    stacked = jnp.concatenate(pieces, axis=-1)
    return stacked.reshape(-1, stacked.shape[-1])


def to_blocks(volume):
    shape = volume.shape
    folded = volume.reshape(
        shape[0], shape[1] // 2, 2, shape[2] // 2, 2, shape[3] // 2, 2, shape[4]
    )
    folded = folded.transpose(0, 1, 3, 5, 2, 4, 6, 7)
    return folded.reshape(-1, 8 * shape[4])


def from_blocks(blocked, shape):
    folded = blocked.reshape(
        shape[0], shape[1] // 2, shape[2] // 2, shape[3] // 2, 2, 2, 2, shape[4]
    )
    folded = folded.transpose(0, 1, 4, 2, 5, 3, 6, 7)
    return folded.reshape(shape)


def flip_taps(w_conv):
    width_in = w_conv.shape[1]
    return (
        w_conv.reshape(27, width_in, width_in)[::-1]
        .transpose(0, 2, 1)
        .reshape(27 * width_in, width_in)
    )


def deep_level(hidden, upstream, w_down, w_up):
    width_in = hidden.shape[-1]
    width_deep = w_down.shape[1]
    hid_blocks = to_blocks(hidden)
    up_blocks = to_blocks(upstream)
    pre_deep = jnp.dot(hid_blocks, w_down, preferred_element_type=jnp.float32)
    deep_act = jax.nn.silu(pre_deep).astype(jnp.bfloat16)
    w_up_back = (
        w_up.reshape(8, width_deep, width_in).transpose(0, 2, 1).reshape(8 * width_in, width_deep)
    )
    grad_act = jnp.dot(up_blocks, w_up_back, preferred_element_type=jnp.float32)
    grad_up = lax.dot_general(
        deep_act, up_blocks, (((0,), (0,)), ((), ())), preferred_element_type=jnp.float32
    )
    grad_up = (
        grad_up.reshape(width_deep, 8, width_in)
        .transpose(1, 0, 2)
        .reshape(8 * width_deep, width_in)
    )
    grad_deep = (grad_act * silu_slope(pre_deep)).astype(jnp.bfloat16)
    grad_down = lax.dot_general(
        hid_blocks, grad_deep, (((0,), (0,)), ((), ())), preferred_element_type=jnp.float32
    )
    back_blocks = jnp.dot(grad_deep, w_down.T, preferred_element_type=jnp.float32).astype(
        jnp.bfloat16
    )
    return (grad_down, grad_up, from_blocks(back_blocks, hidden.shape))


def per_device(inputs, cotangent, w_conv, w_down, w_up):
    width_in = w_conv.shape[1]
    edge_pad = ((0, 0), (0, 0), (1, 1), (1, 1), (0, 0))
    slab_in = extended(inputs, (("sp", 1),), 1)
    columns = unfold_taps(jnp.pad(slab_in, edge_pad))
    pre_conv = jnp.dot(columns, w_conv, preferred_element_type=jnp.float32)
    hidden = jax.nn.silu(pre_conv).astype(jnp.bfloat16).reshape(inputs.shape)
    hidden_crops, upstream_crops = (
        lax.all_to_all(hidden, "sp", split_axis=0, concat_axis=1, tiled=True),
        lax.all_to_all(cotangent, "sp", split_axis=0, concat_axis=1, tiled=True),
    )
    grad_down, grad_up, back_down = deep_level(hidden_crops, upstream_crops, w_down, w_up)
    back_slab = lax.all_to_all(back_down, "sp", split_axis=1, concat_axis=0, tiled=True)
    summed = cotangent.astype(jnp.float32).reshape(-1, width_in) + back_slab.astype(
        jnp.float32
    ).reshape(-1, width_in)
    grad_pre = (summed * silu_slope(pre_conv)).astype(jnp.bfloat16)
    grad_conv = lax.dot_general(
        columns, grad_pre, (((0,), (0,)), ((), ())), preferred_element_type=jnp.float32
    )
    padded_grad = extended(grad_pre.reshape(inputs.shape), (("sp", 1),), 1)
    grad_input = jnp.dot(
        unfold_taps(jnp.pad(padded_grad, edge_pad)),
        flip_taps(w_conv),
        preferred_element_type=jnp.float32,
    )
    grad_input = grad_input.astype(jnp.bfloat16).reshape(inputs.shape)
    local_sums = jnp.concatenate(
        [grad_conv.reshape(-1), grad_down.reshape(-1), grad_up.reshape(-1)]
    )
    within_group = lax.psum(local_sums.astype(jnp.bfloat16), "sp").astype(jnp.float32)
    grad_share = lax.psum_scatter(within_group, "dp", scatter_dimension=0, tiled=True)
    edge_cells = inputs.shape[2]
    crop_total = inputs.shape[0] * lax.axis_size("dp")
    norm_factor = 1.0 / jnp.sqrt(jnp.float32(crop_total * edge_cells * edge_cells * edge_cells))
    return (grad_input, grad_share * norm_factor)


def swap_x(value):
    return lax.ppermute(value, "sp", [(0, 1), (1, 0)])


def swap_dp(value, mask, odd_mask=None):
    masks = (mask, mask if odd_mask is None else odd_mask)
    return lax.ppermute(value, "dp", [(i, i ^ masks[i % 2]) for i in range(16)])


def pick(value, dim, index):
    return lax.dynamic_index_in_dim(value, index, dim, keepdims=False)


ORDER = ((1, 3), (2, 1), (3, 2))


def square_sum(pieces, own):
    received = [
        swap_dp(piece, 2 * even, 2 * odd) for piece, (even, odd) in zip(pieces, ORDER)
    ]
    for part in received:
        own += part.astype(jnp.float32)
    return own


def end_sum(square, scale, pieces):
    far = (lax.axis_index("dp") >> 3) & 1
    side = lax.axis_index("sp")
    sent = pick(square, 0, 1 - far).astype(jnp.bfloat16)
    kept = pick(square, 0, far)
    lows, highs = [], []
    received = [swap_dp(sent[first:last], 8) for first, last in pieces]
    for (first, last), part in zip(pieces, received):
        total = (kept[first:last] + part.astype(jnp.float32)).astype(jnp.bfloat16)
        other = swap_x(total)
        lows.append(jnp.where(side == 0, total, other).astype(jnp.float32) * scale)
        highs.append(jnp.where(side == 0, other, total).astype(jnp.float32) * scale)
    return lows, highs


LANES = 128
VMEM = pl.BlockSpec(memory_space=pltpu.VMEM)
BF16, F32 = jnp.bfloat16, jnp.float32
SHARE = 472
HALF = 240
PLACES = tuple((i, j, k) for i in range(2) for j in range(2) for k in range(2))


def dot(a, b):
    return jnp.dot(a, b, preferred_element_type=F32)


def against(a, b):
    return lax.dot_general(a, b, (((1,), (1,)), ((), ())), preferred_element_type=F32)


def across(parts):
    return jnp.concatenate(parts, axis=-1)


def split_parity(slab_ref, natural_ref):
    for crop in range(2):
        natural_ref[:, :, 8 * crop : 8 * crop + 8, :] = slab_ref[crop].astype(F32)
    return [natural_ref[:, :, pl.ds(parity, 8, stride=2), :] for parity in range(2)]


def fill_taps(taps_ref, even, odd):
    planes = even.shape[0]
    kk = lax.broadcasted_iota(jnp.int32, even.shape, 2) % 4
    before = jnp.where(kk == 0, 0.0, pltpu.roll(odd, 1, 2))
    after = jnp.where(kk == 3, 0.0, pltpu.roll(even, 7, 2))
    for tap, (low, high) in enumerate(((before, even), (even, odd), (odd, after))):
        taps_ref[1 : 1 + planes, pl.ds(1, 8), :, tap * LANES : (tap + 1) * LANES] = jnp.concatenate(
            [low, high], axis=2
        ).astype(BF16)


def clear_rim(taps_ref, with_planes):
    planes, rows, tile, lanes = taps_ref.shape
    row = jnp.zeros((planes, tile, lanes), BF16)
    taps_ref[:, 0] = row
    taps_ref[:, rows - 1] = row
    if with_planes:
        plane = jnp.zeros((rows, tile, lanes), BF16)
        taps_ref[0] = plane
        taps_ref[planes - 1] = plane


def slab_conv(slab_ref, w_ref, natural_ref, taps_ref):
    even, odd = split_parity(slab_ref, natural_ref)
    clear_rim(taps_ref, False)
    fill_taps(taps_ref, even, odd)
    planes = even.shape[0]
    size = planes * 128
    wide = 3 * LANES
    centre = taps_ref[1 : 1 + planes, 1:9, :, LANES : 2 * LANES].reshape(size, LANES)
    turned = centre.astype(F32).T.astype(BF16)
    cells = across([taps_ref[1 : 1 + planes, j : j + 8].reshape(size, wide) for j in range(3)])

    def weights(i):
        return w_ref[i * 3 * wide : (i + 1) * 3 * wide, :]

    first = dot(cells, across([weights(0), weights(1)])).reshape(planes, 128, 2 * LANES)
    last = dot(cells, weights(2)).reshape(planes, 128, LANES)
    none = jnp.zeros((1, 128, LANES), F32)
    two = jnp.zeros((2, 128, LANES), F32)
    added = (
        jnp.concatenate([two, first[:, :, :LANES]])
        + jnp.concatenate([none, first[:, :, LANES:], none])
        + jnp.concatenate([last, two])
    )
    return added, turned


def blocks(parts, tap):
    i, j, k = PLACES[tap]
    even_odd = parts[k]
    planes = even_odd.shape[0]
    folded = even_odd.reshape(planes // 2, 2, 4, 2, 8, LANES)
    return folded[:, i, :, j].reshape(planes * 16, LANES)


def deep_gradient(parts, w_up_ref):
    upstream = across([blocks(parts, tap).astype(BF16) for tap in range(8)])
    deep = w_up_ref.shape[0] // 8
    w_up = across([w_up_ref[tap * deep : (tap + 1) * deep, :] for tap in range(8)])
    return upstream, against(upstream, w_up)


def own_kernel(in_ref, w_ref, add_ref, turned_ref, natural_ref, taps_ref):
    add_ref[...], turned_ref[...] = slab_conv(in_ref, w_ref, natural_ref, taps_ref)


def forward_kernel(
    in_ref,
    w_ref,
    add_ref,
    turned_own_ref,
    w_down_ref,
    up_ref,
    w_up_ref,
    slope_ref,
    turned_ref,
    hidden_ref,
    act_ref,
    deep_slope_ref,
    blocks_own_ref,
    act_own_ref,
    natural_ref,
    taps_ref,
    sum_ref,
):
    side = lax.axis_index("sp")
    planes = in_ref.shape[1]
    added, turned = slab_conv(in_ref, w_ref, natural_ref, taps_ref)
    sum_ref[...] = jnp.zeros_like(sum_ref)
    sum_ref[pl.ds(side * planes, planes + 2)] = add_ref[...]
    sum_ref[pl.ds((1 - side) * planes, planes + 2)] += added
    turned_ref[side] = turned_own_ref[...]
    turned_ref[1 - side] = turned
    folded = (planes, 2, 4, 2, 2, 8, LANES)
    pre = sum_ref[1 : 1 + 2 * planes].reshape(folded)
    sigmoid_value = jax.nn.sigmoid(pre)
    slope_ref[...] = sigmoid_value * (1.0 + pre * (1.0 - sigmoid_value))
    act = pre * sigmoid_value
    hidden = across([act[:, i, :, j, k].reshape(128, LANES).astype(BF16) for i, j, k in PLACES])
    hidden_ref[...] = hidden.astype(F32).T.astype(BF16)
    pre_deep = dot(hidden, w_down_ref[...])
    act_ref[...] = jax.nn.silu(pre_deep).T.astype(BF16)
    deep_slope_ref[...] = silu_slope(pre_deep)
    blocks_own_ref[...], act_own_ref[...] = deep_gradient(
        split_parity(up_ref, natural_ref), w_up_ref
    )


def backward_kernel(
    up_ref,
    slope_ref,
    turned_ref,
    hidden_ref,
    deep_act_ref,
    deep_slope_ref,
    blocks_own_ref,
    act_own_ref,
    w_down_ref,
    w_up_ref,
    mine_ref,
    passed_ref,
    slab_ref,
    taps_ref,
    down_ref,
    natural_ref,
    blocks_ref,
    act_ref,
    folded_ref,
    rows_ref,
):
    side = lax.axis_index("sp")
    core = lax.axis_index("dp") % 2
    parts = split_parity(up_ref, natural_ref)
    upstream, grad_act = deep_gradient(parts, w_up_ref)
    blocks_ref[side] = blocks_own_ref[...]
    blocks_ref[1 - side] = upstream
    act_ref[side] = act_own_ref[...]
    act_ref[1 - side] = grad_act
    upstream = blocks_ref[...].reshape(128, 8 * LANES)
    grad_deep = (act_ref[...].reshape(deep_slope_ref.shape) * deep_slope_ref[...]).astype(BF16)
    back = against(grad_deep, w_down_ref[...]).astype(BF16).astype(F32)
    for tap, (i, j, k) in enumerate(PLACES):
        lanes = slice(tap * LANES, (tap + 1) * LANES)
        summed = (upstream[:, lanes].astype(F32) + back[:, lanes]).reshape(4, 4, 8, LANES)
        folded_ref[:, i, :, j, k] = summed * slope_ref[:, i, :, j, k]
    planes = 8
    whole = (planes, 8, 8, LANES)
    clear_rim(taps_ref, True)
    fill_taps(
        taps_ref,
        folded_ref[:, :, :, :, 0].reshape(whole),
        folded_ref[:, :, :, :, 1].reshape(whole),
    )
    slab_ref[...] = taps_ref[
        pl.ds(side * (planes // 2), planes // 2 + 2), 1:9, :, LANES : 2 * LANES
    ]

    deep = deep_act_ref.shape[0]
    grad_up = dot(deep_act_ref[...], upstream)
    down_at = 27 * LANES
    up_at = down_at + 8 * deep
    for tap in range(8):
        rows_ref[up_at + tap * deep : up_at + (tap + 1) * deep, :] = grad_up[
            :, tap * LANES : (tap + 1) * LANES
        ]
    grad_down = dot(hidden_ref[...], grad_deep)
    for part in range(deep // LANES):
        rows_ref[pl.ds(down_at + part, 8 * LANES, stride=deep // LANES), :] = grad_down[
            :, part * LANES : (part + 1) * LANES
        ]
    down_ref[...] = rows_ref[down_at : down_at + down_ref.shape[0], :]

    def give(own_side, other):
        conv_rows(own_side, other, turned_ref, taps_ref, rows_ref)
        keep_rows(own_side, other, range(8), rows_ref, passed_ref)
        keep_rows(own_side, 1 - other, range(4, 8), rows_ref, mine_ref)

    for_place(side, 1 - core, give)


def for_place(side, owner, body):
    for own_side in range(2):
        for own_owner in range(2):
            pl.when((side == own_side) & (owner == own_owner))(
                functools.partial(body, own_side, own_owner)
            )


def window(side, owner, pair):
    return (2 * pair + owner) * SHARE + side * (SHARE - HALF)


def conv_rows(side, owner, turned_ref, taps_ref, rows_ref):
    starts = [window(side, owner, pair) for pair in range(8)]
    kept = [
        tap
        for tap in range(27)
        if any(at < (tap + 1) * LANES and tap * LANES < at + HALF for at in starts)
    ]
    turned = across([turned_ref[0], turned_ref[1]])
    planes = taps_ref.shape[0] - 2
    size = planes * 128
    cells = []
    for tap in kept:
        i, j, k = (26 - tap) // 9, (26 - tap) // 3 % 3, (26 - tap) % 3
        cells.append(
            taps_ref[i : i + planes, j : j + 8, :, k * LANES : (k + 1) * LANES].reshape(size, LANES)
        )
    sums = dot(turned, across(cells))
    for at, tap in enumerate(kept):
        rows_ref[tap * LANES : (tap + 1) * LANES, :] = sums[:, at * LANES : (at + 1) * LANES]


def keep_rows(side, owner, pairs, rows_ref, target_ref):
    for at, pair in enumerate(pairs):
        first = window(side, owner, pair)
        target_ref[at] = rows_ref[first : first + HALF, :].astype(BF16)


def own_rows_kernel(taps_ref, turned_ref, down_ref, mine_ref, rows_ref):
    rows_ref[27 * LANES :, :] = down_ref[...]

    def give(own_side, own_core):
        conv_rows(own_side, own_core, turned_ref, taps_ref, rows_ref)
        keep_rows(own_side, own_core, range(4), rows_ref, mine_ref)

    for_place(lax.axis_index("sp"), lax.axis_index("dp") % 2, give)


def chip_kernel(late_ref, early_ref, passed_ref, first_ref, second_ref, third_ref, own_ref):
    at = lax.axis_index("dp")
    here = (at >> 1) & 3
    odd_core = at & 1

    def chip_sum(far, index):
        mine = (late_ref, early_ref)[far][index]
        return mine.astype(F32) + passed_ref[4 * far + index].astype(F32)

    for far in range(2):
        for target, (even, odd) in zip((first_ref, second_ref, third_ref), ORDER):
            index = here ^ (even + odd_core * (odd - even))
            target[far] = chip_sum(far, index).astype(BF16)
        own_ref[far] = chip_sum(far, here)


def input_kernel(slab_ref, w_ref, out_ref, taps_ref, natural_ref):
    slab = slab_ref[...].astype(F32)
    own = slab.shape[0] - 2
    size = own * 128
    clear_rim(taps_ref, False)
    fill_taps(taps_ref, slab[:, :, :8], slab[:, :, 8:])
    total = jnp.zeros((size, LANES), F32)
    for i in range(3):
        for j in range(3):
            first = 26 - 9 * i - 3 * j
            weights = across(
                [w_ref[(first - k) * LANES : (first - k + 1) * LANES, :] for k in range(3)]
            )
            cells = taps_ref[1 + i : 1 + i + own, j : j + 8].reshape(size, 3 * LANES)
            total += against(cells, weights)
    total = total.reshape(own, 8, 2, 8, LANES)
    for parity in range(2):
        natural_ref[:, :, pl.ds(parity, 8, stride=2), :] = total[:, :, parity]
    for crop in range(2):
        out_ref[crop] = natural_ref[:, :, 8 * crop : 8 * crop + 8, :].astype(BF16)


def run(body, operands, outs, scratch, flops):
    return pl.pallas_call(
        body,
        out_shape=tuple(jax.ShapeDtypeStruct(shape, kind) for shape, kind in outs),
        in_specs=[VMEM] * len(operands),
        out_specs=(VMEM,) * len(outs),
        scratch_shapes=[pltpu.VMEM(shape, kind) for shape, kind in scratch],
        compiler_params=pltpu.CompilerParams(vmem_limit_bytes=40 << 20),
        cost_estimate=pl.CostEstimate(flops=flops, bytes_accessed=1 << 21, transcendentals=0),
    )(*operands)


def per_device_pairs(inputs, cotangent, w_conv, w_down, w_up):
    deep = w_down.shape[1]
    other_in = swap_x(inputs)
    other_up = swap_x(cotangent)
    natural = ((4, 8, 16, LANES), F32)
    slab_taps = ((6, 10, 16, 3 * LANES), BF16)
    blocked = ((64, 8 * LANES), BF16)
    act = ((64, deep), F32)
    added, turned_own = run(
        own_kernel,
        (inputs, w_conv),
        [((6, 128, LANES), F32), ((LANES, 512), BF16)],
        [natural, slab_taps],
        10**9,
    )
    folded = ((4, 2, 4, 2, 2, 8, LANES), F32)
    saved = run(
        forward_kernel,
        (other_in, w_conv, added, turned_own, w_down, cotangent, w_up),
        [
            folded,
            ((2, LANES, 512), BF16),
            ((8 * LANES, 128), BF16),
            ((deep, 128), BF16),
            ((128, deep), F32),
            blocked,
            act,
        ],
        [natural, slab_taps, ((10, 128, LANES), F32)],
        10**9,
    )
    total_rows = (w_conv.size + w_down.size + w_up.size) // LANES
    conv_count = w_conv.size // LANES
    taps = ((10, 10, 16, 3 * LANES), BF16)
    given = ((4, HALF, LANES), BF16)
    down = ((8 * SHARE - conv_count, LANES), F32)
    early_mine, passed, slab, grad_taps, down_rows = run(
        backward_kernel,
        (other_up, *saved, w_down, w_up),
        [given, ((8, HALF, LANES), BF16), ((6, 8, 16, LANES), BF16), taps, down],
        [
            natural,
            ((2, *blocked[0]), BF16),
            ((2, *act[0]), F32),
            folded,
            ((total_rows, LANES), F32),
        ],
        10**9,
    )
    (late_mine,) = run(
        own_rows_kernel,
        (grad_taps, saved[1], down_rows),
        [given],
        [((8 * SHARE, LANES), F32)],
        10**9,
    )
    (grad_input,) = run(
        input_kernel,
        (slab, w_conv),
        [(inputs.shape, BF16)],
        [((8, 10, 16, 3 * LANES), BF16), natural],
        10**9,
    )

    piece = ((2, HALF, LANES), BF16)
    *pieces, own = run(
        chip_kernel,
        (late_mine, early_mine, swap_dp(passed, 1)),
        [piece, piece, piece, (piece[0], F32)],
        [],
        10**6,
    )
    square = square_sum(pieces, own)
    crop_total = inputs.shape[0] * lax.axis_size("dp")
    scale = 1.0 / jnp.sqrt(jnp.float32(crop_total * inputs.shape[2] ** 3))
    lows, highs = end_sum(square, scale, ((0, HALF),))
    highs[0] = highs[0][2 * HALF - SHARE :]
    grad_share = jnp.concatenate(lows + highs).reshape(-1)
    return (grad_input, grad_share)


def solution(mesh):
    pairs = dict(mesh.shape) == {"sp": 2, "dp": 16}
    return jax.shard_map(
        per_device_pairs if pairs else per_device,
        mesh=mesh,
        in_specs=(P("dp", "sp", None, None, None), P("dp", "sp", None, None, None), P(), P(), P()),
        out_specs=(P("dp", "sp", None, None, None), P("dp")),
        check_vma=False,
    )
```

```python
import functools

import jax
import jax.numpy as jnp
from jax import lax
from jax.experimental import pallas as pl
from jax.experimental.pallas import tpu as pltpu
from jax.sharding import PartitionSpec as P


def extended(cells, sides, width):
    for axis, dim in sides:
        count = lax.axis_size(axis)
        ends = count - 1
        head = lax.slice_in_dim(cells, 0, width, axis=dim)
        tail = lax.slice_in_dim(cells, cells.shape[dim] - width, cells.shape[dim], axis=dim)
        cells = jnp.concatenate(
            [
                lax.ppermute(tail, axis, [(i, (i + 1) % count) for i in range(ends)]),
                cells,
                lax.ppermute(head, axis, [((i + 1) % count, i) for i in range(ends)]),
            ],
            axis=dim,
        )
    return cells


def silu_slope(pre_act):
    sigmoid_value = jax.nn.sigmoid(pre_act)
    return sigmoid_value * (1.0 + pre_act * (1.0 - sigmoid_value))


def unfold_taps(padded):
    first_size = padded.shape[1] - 2
    second_size = padded.shape[2] - 2
    third_size = padded.shape[3] - 2
    pieces = [
        padded[:, i : i + first_size, j : j + second_size, k : k + third_size, :]
        for i in range(3)
        for j in range(3)
        for k in range(3)
    ]
    stacked = jnp.concatenate(pieces, axis=-1)
    return stacked.reshape(-1, stacked.shape[-1])


def to_blocks(volume):
    shape = volume.shape
    folded = volume.reshape(
        shape[0], shape[1] // 2, 2, shape[2] // 2, 2, shape[3] // 2, 2, shape[4]
    )
    folded = folded.transpose(0, 1, 3, 5, 2, 4, 6, 7)
    return folded.reshape(-1, 8 * shape[4])


def from_blocks(blocked, shape):
    folded = blocked.reshape(
        shape[0], shape[1] // 2, shape[2] // 2, shape[3] // 2, 2, 2, 2, shape[4]
    )
    folded = folded.transpose(0, 1, 4, 2, 5, 3, 6, 7)
    return folded.reshape(shape)


def flip_taps(w_conv):
    width_in = w_conv.shape[1]
    return (
        w_conv.reshape(27, width_in, width_in)[::-1]
        .transpose(0, 2, 1)
        .reshape(27 * width_in, width_in)
    )


def deep_level(hidden, upstream, w_down, w_up):
    width_in = hidden.shape[-1]
    width_deep = w_down.shape[1]
    hid_blocks = to_blocks(hidden)
    up_blocks = to_blocks(upstream)
    pre_deep = jnp.dot(hid_blocks, w_down, preferred_element_type=jnp.float32)
    deep_act = jax.nn.silu(pre_deep).astype(jnp.bfloat16)
    w_up_back = (
        w_up.reshape(8, width_deep, width_in).transpose(0, 2, 1).reshape(8 * width_in, width_deep)
    )
    grad_act = jnp.dot(up_blocks, w_up_back, preferred_element_type=jnp.float32)
    grad_up = lax.dot_general(
        deep_act, up_blocks, (((0,), (0,)), ((), ())), preferred_element_type=jnp.float32
    )
    grad_up = (
        grad_up.reshape(width_deep, 8, width_in)
        .transpose(1, 0, 2)
        .reshape(8 * width_deep, width_in)
    )
    grad_deep = (grad_act * silu_slope(pre_deep)).astype(jnp.bfloat16)
    grad_down = lax.dot_general(
        hid_blocks, grad_deep, (((0,), (0,)), ((), ())), preferred_element_type=jnp.float32
    )
    back_blocks = jnp.dot(grad_deep, w_down.T, preferred_element_type=jnp.float32).astype(
        jnp.bfloat16
    )
    return (grad_down, grad_up, from_blocks(back_blocks, hidden.shape))


def per_device(inputs, cotangent, w_conv, w_down, w_up):
    width_in = w_conv.shape[1]
    edge_pad = ((0, 0), (0, 0), (1, 1), (1, 1), (0, 0))
    slab_in = extended(inputs, (("sp", 1),), 1)
    columns = unfold_taps(jnp.pad(slab_in, edge_pad))
    pre_conv = jnp.dot(columns, w_conv, preferred_element_type=jnp.float32)
    hidden = jax.nn.silu(pre_conv).astype(jnp.bfloat16).reshape(inputs.shape)
    hidden_crops, upstream_crops = (
        lax.all_to_all(hidden, "sp", split_axis=0, concat_axis=1, tiled=True),
        lax.all_to_all(cotangent, "sp", split_axis=0, concat_axis=1, tiled=True),
    )
    grad_down, grad_up, back_down = deep_level(hidden_crops, upstream_crops, w_down, w_up)
    back_slab = lax.all_to_all(back_down, "sp", split_axis=1, concat_axis=0, tiled=True)
    summed = cotangent.astype(jnp.float32).reshape(-1, width_in) + back_slab.astype(
        jnp.float32
    ).reshape(-1, width_in)
    grad_pre = (summed * silu_slope(pre_conv)).astype(jnp.bfloat16)
    grad_conv = lax.dot_general(
        columns, grad_pre, (((0,), (0,)), ((), ())), preferred_element_type=jnp.float32
    )
    padded_grad = extended(grad_pre.reshape(inputs.shape), (("sp", 1),), 1)
    grad_input = jnp.dot(
        unfold_taps(jnp.pad(padded_grad, edge_pad)),
        flip_taps(w_conv),
        preferred_element_type=jnp.float32,
    )
    grad_input = grad_input.astype(jnp.bfloat16).reshape(inputs.shape)
    local_sums = jnp.concatenate(
        [grad_conv.reshape(-1), grad_down.reshape(-1), grad_up.reshape(-1)]
    )
    within_group = lax.psum(local_sums.astype(jnp.bfloat16), "sp").astype(jnp.float32)
    grad_share = lax.psum_scatter(within_group, "dp", scatter_dimension=0, tiled=True)
    edge_cells = inputs.shape[2]
    crop_total = inputs.shape[0] * lax.axis_size("dp")
    norm_factor = 1.0 / jnp.sqrt(jnp.float32(crop_total * edge_cells * edge_cells * edge_cells))
    return (grad_input, grad_share * norm_factor)


def swap_x(value):
    return lax.ppermute(value, "sp", [(0, 1), (1, 0)])


def swap_dp(value, mask, odd_mask=None):
    masks = (mask, mask if odd_mask is None else odd_mask)
    return lax.ppermute(value, "dp", [(i, i ^ masks[i % 2]) for i in range(16)])


def pick(value, dim, index):
    return lax.dynamic_index_in_dim(value, index, dim, keepdims=False)


ORDER = ((1, 3), (2, 1), (3, 2))


def square_sum(pieces, own):
    received = [
        swap_dp(piece, 2 * even, 2 * odd) for piece, (even, odd) in zip(pieces, ORDER)
    ]
    for part in received:
        own += part.astype(jnp.float32)
    return own


def end_sum(square, scale, pieces):
    far = (lax.axis_index("dp") >> 3) & 1
    side = lax.axis_index("sp")
    sent = pick(square, 0, 1 - far).astype(jnp.bfloat16)
    kept = pick(square, 0, far)
    lows, highs = [], []
    received = [swap_dp(sent[first:last], 8) for first, last in pieces]
    for (first, last), part in zip(pieces, received):
        total = (kept[first:last] + part.astype(jnp.float32)).astype(jnp.bfloat16)
        other = swap_x(total)
        lows.append(jnp.where(side == 0, total, other).astype(jnp.float32) * scale)
        highs.append(jnp.where(side == 0, other, total).astype(jnp.float32) * scale)
    return lows, highs


LANES = 128
VMEM = pl.BlockSpec(memory_space=pltpu.VMEM)
BF16, F32 = jnp.bfloat16, jnp.float32
SHARE = 472
HALF = 240
EARLY = 2
PLACES = tuple((i, j, k) for i in range(2) for j in range(2) for k in range(2))


def dot(a, b):
    return jnp.dot(a, b, preferred_element_type=F32)


def against(a, b):
    return lax.dot_general(a, b, (((1,), (1,)), ((), ())), preferred_element_type=F32)


def across(parts):
    return jnp.concatenate(parts, axis=-1)


def split_parity(slab_ref, natural_ref):
    for crop in range(2):
        natural_ref[:, :, 8 * crop : 8 * crop + 8, :] = slab_ref[crop].astype(F32)
    return [natural_ref[:, :, pl.ds(parity, 8, stride=2), :] for parity in range(2)]


def fill_taps(taps_ref, even, odd):
    planes = even.shape[0]
    kk = lax.broadcasted_iota(jnp.int32, even.shape, 2) % 4
    before = jnp.where(kk == 0, 0.0, pltpu.roll(odd, 1, 2))
    after = jnp.where(kk == 3, 0.0, pltpu.roll(even, 7, 2))
    for tap, (low, high) in enumerate(((before, even), (even, odd), (odd, after))):
        taps_ref[1 : 1 + planes, pl.ds(1, 8), :, tap * LANES : (tap + 1) * LANES] = jnp.concatenate(
            [low, high], axis=2
        ).astype(BF16)


def clear_rim(taps_ref, with_planes):
    planes, rows, tile, lanes = taps_ref.shape
    row = jnp.zeros((planes, tile, lanes), BF16)
    taps_ref[:, 0] = row
    taps_ref[:, rows - 1] = row
    if with_planes:
        plane = jnp.zeros((rows, tile, lanes), BF16)
        taps_ref[0] = plane
        taps_ref[planes - 1] = plane


def slab_conv(slab_ref, w_ref, natural_ref, taps_ref):
    even, odd = split_parity(slab_ref, natural_ref)
    clear_rim(taps_ref, False)
    fill_taps(taps_ref, even, odd)
    planes = even.shape[0]
    size = planes * 128
    wide = 3 * LANES
    centre = taps_ref[1 : 1 + planes, 1:9, :, LANES : 2 * LANES].reshape(size, LANES)
    turned = centre.astype(F32).T.astype(BF16)
    cells = across([taps_ref[1 : 1 + planes, j : j + 8].reshape(size, wide) for j in range(3)])

    def weights(i):
        return w_ref[i * 3 * wide : (i + 1) * 3 * wide, :]

    first = dot(cells, across([weights(0), weights(1)])).reshape(planes, 128, 2 * LANES)
    last = dot(cells, weights(2)).reshape(planes, 128, LANES)
    none = jnp.zeros((1, 128, LANES), F32)
    two = jnp.zeros((2, 128, LANES), F32)
    added = (
        jnp.concatenate([two, first[:, :, :LANES]])
        + jnp.concatenate([none, first[:, :, LANES:], none])
        + jnp.concatenate([last, two])
    )
    return added, turned


def blocks(parts, tap):
    i, j, k = PLACES[tap]
    even_odd = parts[k]
    planes = even_odd.shape[0]
    folded = even_odd.reshape(planes // 2, 2, 4, 2, 8, LANES)
    return folded[:, i, :, j].reshape(planes * 16, LANES)


def deep_gradient(parts, w_up_ref):
    upstream = across([blocks(parts, tap).astype(BF16) for tap in range(8)])
    deep = w_up_ref.shape[0] // 8
    w_up = across([w_up_ref[tap * deep : (tap + 1) * deep, :] for tap in range(8)])
    return upstream, against(upstream, w_up)


def own_kernel(in_ref, w_ref, add_ref, turned_ref, natural_ref, taps_ref):
    add_ref[...], turned_ref[...] = slab_conv(in_ref, w_ref, natural_ref, taps_ref)


def forward_kernel(
    in_ref,
    w_ref,
    add_ref,
    turned_own_ref,
    w_down_ref,
    up_ref,
    w_up_ref,
    slope_ref,
    turned_ref,
    hidden_ref,
    act_ref,
    deep_slope_ref,
    blocks_own_ref,
    act_own_ref,
    natural_ref,
    taps_ref,
    sum_ref,
):
    side = lax.axis_index("sp")
    planes = in_ref.shape[1]
    added, turned = slab_conv(in_ref, w_ref, natural_ref, taps_ref)
    sum_ref[...] = jnp.zeros_like(sum_ref)
    sum_ref[pl.ds(side * planes, planes + 2)] = add_ref[...]
    sum_ref[pl.ds((1 - side) * planes, planes + 2)] += added
    turned_ref[side] = turned_own_ref[...]
    turned_ref[1 - side] = turned
    folded = (planes, 2, 4, 2, 2, 8, LANES)
    pre = sum_ref[1 : 1 + 2 * planes].reshape(folded)
    sigmoid_value = jax.nn.sigmoid(pre)
    slope_ref[...] = sigmoid_value * (1.0 + pre * (1.0 - sigmoid_value))
    act = pre * sigmoid_value
    hidden = across([act[:, i, :, j, k].reshape(128, LANES).astype(BF16) for i, j, k in PLACES])
    hidden_ref[...] = hidden.astype(F32).T.astype(BF16)
    pre_deep = dot(hidden, w_down_ref[...])
    act_ref[...] = jax.nn.silu(pre_deep).T.astype(BF16)
    deep_slope_ref[...] = silu_slope(pre_deep)
    blocks_own_ref[...], act_own_ref[...] = deep_gradient(
        split_parity(up_ref, natural_ref), w_up_ref
    )


def backward_kernel(
    up_ref,
    slope_ref,
    turned_ref,
    hidden_ref,
    deep_act_ref,
    deep_slope_ref,
    blocks_own_ref,
    act_own_ref,
    w_down_ref,
    w_up_ref,
    mine_ref,
    first_ref,
    rest_ref,
    slab_ref,
    taps_ref,
    down_ref,
    natural_ref,
    blocks_ref,
    act_ref,
    folded_ref,
    rows_ref,
):
    side = lax.axis_index("sp")
    core = lax.axis_index("dp") % 2
    parts = split_parity(up_ref, natural_ref)
    upstream, grad_act = deep_gradient(parts, w_up_ref)
    blocks_ref[side] = blocks_own_ref[...]
    blocks_ref[1 - side] = upstream
    act_ref[side] = act_own_ref[...]
    act_ref[1 - side] = grad_act
    upstream = blocks_ref[...].reshape(128, 8 * LANES)
    grad_deep = (act_ref[...].reshape(deep_slope_ref.shape) * deep_slope_ref[...]).astype(BF16)
    back = against(grad_deep, w_down_ref[...]).astype(BF16).astype(F32)
    for tap, (i, j, k) in enumerate(PLACES):
        lanes = slice(tap * LANES, (tap + 1) * LANES)
        summed = (upstream[:, lanes].astype(F32) + back[:, lanes]).reshape(4, 4, 8, LANES)
        folded_ref[:, i, :, j, k] = summed * slope_ref[:, i, :, j, k]
    planes = 8
    whole = (planes, 8, 8, LANES)
    clear_rim(taps_ref, True)
    fill_taps(
        taps_ref,
        folded_ref[:, :, :, :, 0].reshape(whole),
        folded_ref[:, :, :, :, 1].reshape(whole),
    )
    slab_ref[...] = taps_ref[
        pl.ds(side * (planes // 2), planes // 2 + 2), 1:9, :, LANES : 2 * LANES
    ]

    deep = deep_act_ref.shape[0]
    grad_up = dot(deep_act_ref[...], upstream)
    down_at = 27 * LANES
    up_at = down_at + 8 * deep
    for tap in range(8):
        rows_ref[up_at + tap * deep : up_at + (tap + 1) * deep, :] = grad_up[
            :, tap * LANES : (tap + 1) * LANES
        ]
    grad_down = dot(hidden_ref[...], grad_deep)
    for part in range(deep // LANES):
        rows_ref[pl.ds(down_at + part, 8 * LANES, stride=deep // LANES), :] = grad_down[
            :, part * LANES : (part + 1) * LANES
        ]
    down_ref[...] = rows_ref[down_at : down_at + down_ref.shape[0], :]
    here = (lax.axis_index("dp") >> 1) & 3

    def give(own_side, other):
        conv_rows(own_side, other, turned_ref, taps_ref, rows_ref)
        steps = [step[other] for step in ORDER] + [0]
        for far in range(2):
            for place, step in enumerate(steps):
                start = window(own_side, other, 4 * far + (here ^ step))
                target, slot = (first_ref, place) if place < EARLY else (rest_ref, place - EARLY)
                target[2 * slot + far] = rows_ref[
                    pl.ds(pl.multiple_of(start, 8), HALF), :
                ].astype(BF16)
        keep_rows(own_side, 1 - other, range(4, 8), rows_ref, mine_ref)

    for_place(side, 1 - core, give)


def for_place(side, owner, body):
    for own_side in range(2):
        for own_owner in range(2):
            pl.when((side == own_side) & (owner == own_owner))(
                functools.partial(body, own_side, own_owner)
            )


def window(side, owner, pair):
    return (2 * pair + owner) * SHARE + side * (SHARE - HALF)


def conv_rows(side, owner, turned_ref, taps_ref, rows_ref):
    starts = [window(side, owner, pair) for pair in range(8)]
    kept = [
        tap
        for tap in range(27)
        if any(at < (tap + 1) * LANES and tap * LANES < at + HALF for at in starts)
    ]
    turned = across([turned_ref[0], turned_ref[1]])
    planes = taps_ref.shape[0] - 2
    size = planes * 128
    cells = []
    for tap in kept:
        i, j, k = (26 - tap) // 9, (26 - tap) // 3 % 3, (26 - tap) % 3
        cells.append(
            taps_ref[i : i + planes, j : j + 8, :, k * LANES : (k + 1) * LANES].reshape(size, LANES)
        )
    sums = dot(turned, across(cells))
    for at, tap in enumerate(kept):
        rows_ref[tap * LANES : (tap + 1) * LANES, :] = sums[:, at * LANES : (at + 1) * LANES]


def keep_rows(side, owner, pairs, rows_ref, target_ref):
    for at, pair in enumerate(pairs):
        first = window(side, owner, pair)
        target_ref[at] = rows_ref[first : first + HALF, :].astype(BF16)


def own_rows_kernel(taps_ref, turned_ref, down_ref, mine_ref, rows_ref):
    rows_ref[27 * LANES :, :] = down_ref[...]

    def give(own_side, own_core):
        conv_rows(own_side, own_core, turned_ref, taps_ref, rows_ref)
        keep_rows(own_side, own_core, range(4), rows_ref, mine_ref)

    for_place(lax.axis_index("sp"), lax.axis_index("dp") % 2, give)


def chip_kernel(steps, late_ref, early_ref, passed_ref, *targets):
    at = lax.axis_index("dp")
    for place, ((even, odd), target) in enumerate(zip(steps, targets)):
        index = ((at >> 1) & 3) ^ (even + (at & 1) * (odd - even))
        for far, mine_ref in enumerate((late_ref, early_ref)):
            total = mine_ref[index].astype(F32) + passed_ref[2 * place + far].astype(F32)
            target[far] = total.astype(target.dtype)


def input_kernel(slab_ref, w_ref, out_ref, taps_ref, natural_ref):
    slab = slab_ref[...].astype(F32)
    own = slab.shape[0] - 2
    size = own * 128
    clear_rim(taps_ref, False)
    fill_taps(taps_ref, slab[:, :, :8], slab[:, :, 8:])
    total = jnp.zeros((size, LANES), F32)
    for i in range(3):
        for j in range(3):
            first = 26 - 9 * i - 3 * j
            weights = across(
                [w_ref[(first - k) * LANES : (first - k + 1) * LANES, :] for k in range(3)]
            )
            cells = taps_ref[1 + i : 1 + i + own, j : j + 8].reshape(size, 3 * LANES)
            total += against(cells, weights)
    total = total.reshape(own, 8, 2, 8, LANES)
    for parity in range(2):
        natural_ref[:, :, pl.ds(parity, 8, stride=2), :] = total[:, :, parity]
    for crop in range(2):
        out_ref[crop] = natural_ref[:, :, 8 * crop : 8 * crop + 8, :].astype(BF16)


def run(body, operands, outs, scratch, flops):
    return pl.pallas_call(
        body,
        out_shape=tuple(jax.ShapeDtypeStruct(shape, kind) for shape, kind in outs),
        in_specs=[VMEM] * len(operands),
        out_specs=(VMEM,) * len(outs),
        scratch_shapes=[pltpu.VMEM(shape, kind) for shape, kind in scratch],
        compiler_params=pltpu.CompilerParams(vmem_limit_bytes=24 << 20),
        cost_estimate=pl.CostEstimate(flops=flops, bytes_accessed=1 << 21, transcendentals=0),
    )(*operands)


def per_device_pairs(inputs, cotangent, w_conv, w_down, w_up):
    deep = w_down.shape[1]
    other_in = swap_x(inputs)
    other_up = swap_x(cotangent)
    natural = ((4, 8, 16, LANES), F32)
    slab_taps = ((6, 10, 16, 3 * LANES), BF16)
    blocked = ((64, 8 * LANES), BF16)
    act = ((64, deep), F32)
    added, turned_own = run(
        own_kernel,
        (inputs, w_conv),
        [((6, 128, LANES), F32), ((LANES, 512), BF16)],
        [natural, slab_taps],
        10**9,
    )
    folded = ((4, 2, 4, 2, 2, 8, LANES), F32)
    saved = run(
        forward_kernel,
        (other_in, w_conv, added, turned_own, w_down, cotangent, w_up),
        [
            folded,
            ((2, LANES, 512), BF16),
            ((8 * LANES, 128), BF16),
            ((deep, 128), BF16),
            ((128, deep), F32),
            blocked,
            act,
        ],
        [natural, slab_taps, ((10, 128, LANES), F32)],
        10**9,
    )
    total_rows = (w_conv.size + w_down.size + w_up.size) // LANES
    conv_count = w_conv.size // LANES
    taps = ((10, 10, 16, 3 * LANES), BF16)
    given = ((4, HALF, LANES), BF16)
    down = ((8 * SHARE - conv_count, LANES), F32)
    early_mine, first, rest, slab, grad_taps, down_rows = run(
        backward_kernel,
        (other_up, *saved, w_down, w_up),
        [
            given,
            ((2 * EARLY, HALF, LANES), BF16),
            ((8 - 2 * EARLY, HALF, LANES), BF16),
            ((6, 8, 16, LANES), BF16),
            taps,
            down,
        ],
        [
            natural,
            ((2, *blocked[0]), BF16),
            ((2, *act[0]), F32),
            folded,
            ((total_rows, LANES), F32),
        ],
        10**9,
    )
    (late_mine,) = run(
        own_rows_kernel,
        (grad_taps, saved[1], down_rows),
        [given],
        [((8 * SHARE, LANES), F32)],
        10**9,
    )
    (grad_input,) = run(
        input_kernel,
        (slab, w_conv),
        [(inputs.shape, BF16)],
        [((8, 10, 16, 3 * LANES), BF16), natural],
        10**9,
    )

    first, rest = swap_dp(first, 1), swap_dp(rest, 1)
    sums = [((2, HALF, LANES), BF16)] * 3 + [((2, HALF, LANES), F32)]
    steps = (*ORDER, (0, 0))
    *pieces, own = (
        part
        for passed, places in ((first, slice(0, EARLY)), (rest, slice(EARLY, 4)))
        for part in run(
            functools.partial(chip_kernel, steps[places]),
            (late_mine, early_mine, passed),
            sums[places],
            [],
            10**6,
        )
    )
    square = square_sum(pieces, own)
    crop_total = inputs.shape[0] * lax.axis_size("dp")
    scale = 1.0 / jnp.sqrt(jnp.float32(crop_total * inputs.shape[2] ** 3))
    lows, highs = end_sum(square, scale, ((0, HALF),))
    highs[0] = highs[0][2 * HALF - SHARE :]
    grad_share = jnp.concatenate(lows + highs).reshape(-1)
    return (grad_input, grad_share)


def solution(mesh):
    pairs = dict(mesh.shape) == {"sp": 2, "dp": 16}
    return jax.shard_map(
        per_device_pairs if pairs else per_device,
        mesh=mesh,
        in_specs=(P("dp", "sp", None, None, None), P("dp", "sp", None, None, None), P(), P(), P()),
        out_specs=(P("dp", "sp", None, None, None), P("dp")),
        check_vma=False,
    )
```

```python
import functools

import jax
import jax.numpy as jnp
from jax import lax
from jax.experimental import pallas as pl
from jax.experimental.pallas import tpu as pltpu
from jax.sharding import PartitionSpec as P


def extended(cells, sides, width):
    for axis, dim in sides:
        count = lax.axis_size(axis)
        ends = count - 1
        head = lax.slice_in_dim(cells, 0, width, axis=dim)
        tail = lax.slice_in_dim(cells, cells.shape[dim] - width, cells.shape[dim], axis=dim)
        cells = jnp.concatenate(
            [
                lax.ppermute(tail, axis, [(i, (i + 1) % count) for i in range(ends)]),
                cells,
                lax.ppermute(head, axis, [((i + 1) % count, i) for i in range(ends)]),
            ],
            axis=dim,
        )
    return cells


def silu_slope(pre_act):
    sigmoid_value = jax.nn.sigmoid(pre_act)
    return sigmoid_value * (1.0 + pre_act * (1.0 - sigmoid_value))


def unfold_taps(padded):
    first_size = padded.shape[1] - 2
    second_size = padded.shape[2] - 2
    third_size = padded.shape[3] - 2
    pieces = [
        padded[:, i : i + first_size, j : j + second_size, k : k + third_size, :]
        for i in range(3)
        for j in range(3)
        for k in range(3)
    ]
    stacked = jnp.concatenate(pieces, axis=-1)
    return stacked.reshape(-1, stacked.shape[-1])


def to_blocks(volume):
    shape = volume.shape
    folded = volume.reshape(
        shape[0], shape[1] // 2, 2, shape[2] // 2, 2, shape[3] // 2, 2, shape[4]
    )
    folded = folded.transpose(0, 1, 3, 5, 2, 4, 6, 7)
    return folded.reshape(-1, 8 * shape[4])


def from_blocks(blocked, shape):
    folded = blocked.reshape(
        shape[0], shape[1] // 2, shape[2] // 2, shape[3] // 2, 2, 2, 2, shape[4]
    )
    folded = folded.transpose(0, 1, 4, 2, 5, 3, 6, 7)
    return folded.reshape(shape)


def flip_taps(w_conv):
    width_in = w_conv.shape[1]
    return (
        w_conv.reshape(27, width_in, width_in)[::-1]
        .transpose(0, 2, 1)
        .reshape(27 * width_in, width_in)
    )


def deep_level(hidden, upstream, w_down, w_up):
    width_in = hidden.shape[-1]
    width_deep = w_down.shape[1]
    hid_blocks = to_blocks(hidden)
    up_blocks = to_blocks(upstream)
    pre_deep = jnp.dot(hid_blocks, w_down, preferred_element_type=jnp.float32)
    deep_act = jax.nn.silu(pre_deep).astype(jnp.bfloat16)
    w_up_back = (
        w_up.reshape(8, width_deep, width_in).transpose(0, 2, 1).reshape(8 * width_in, width_deep)
    )
    grad_act = jnp.dot(up_blocks, w_up_back, preferred_element_type=jnp.float32)
    grad_up = lax.dot_general(
        deep_act, up_blocks, (((0,), (0,)), ((), ())), preferred_element_type=jnp.float32
    )
    grad_up = (
        grad_up.reshape(width_deep, 8, width_in)
        .transpose(1, 0, 2)
        .reshape(8 * width_deep, width_in)
    )
    grad_deep = (grad_act * silu_slope(pre_deep)).astype(jnp.bfloat16)
    grad_down = lax.dot_general(
        hid_blocks, grad_deep, (((0,), (0,)), ((), ())), preferred_element_type=jnp.float32
    )
    back_blocks = jnp.dot(grad_deep, w_down.T, preferred_element_type=jnp.float32).astype(
        jnp.bfloat16
    )
    return (grad_down, grad_up, from_blocks(back_blocks, hidden.shape))


def per_device(inputs, cotangent, w_conv, w_down, w_up):
    width_in = w_conv.shape[1]
    edge_pad = ((0, 0), (0, 0), (1, 1), (1, 1), (0, 0))
    slab_in = extended(inputs, (("sp", 1),), 1)
    columns = unfold_taps(jnp.pad(slab_in, edge_pad))
    pre_conv = jnp.dot(columns, w_conv, preferred_element_type=jnp.float32)
    hidden = jax.nn.silu(pre_conv).astype(jnp.bfloat16).reshape(inputs.shape)
    hidden_crops, upstream_crops = (
        lax.all_to_all(hidden, "sp", split_axis=0, concat_axis=1, tiled=True),
        lax.all_to_all(cotangent, "sp", split_axis=0, concat_axis=1, tiled=True),
    )
    grad_down, grad_up, back_down = deep_level(hidden_crops, upstream_crops, w_down, w_up)
    back_slab = lax.all_to_all(back_down, "sp", split_axis=1, concat_axis=0, tiled=True)
    summed = cotangent.astype(jnp.float32).reshape(-1, width_in) + back_slab.astype(
        jnp.float32
    ).reshape(-1, width_in)
    grad_pre = (summed * silu_slope(pre_conv)).astype(jnp.bfloat16)
    grad_conv = lax.dot_general(
        columns, grad_pre, (((0,), (0,)), ((), ())), preferred_element_type=jnp.float32
    )
    padded_grad = extended(grad_pre.reshape(inputs.shape), (("sp", 1),), 1)
    grad_input = jnp.dot(
        unfold_taps(jnp.pad(padded_grad, edge_pad)),
        flip_taps(w_conv),
        preferred_element_type=jnp.float32,
    )
    grad_input = grad_input.astype(jnp.bfloat16).reshape(inputs.shape)
    local_sums = jnp.concatenate(
        [grad_conv.reshape(-1), grad_down.reshape(-1), grad_up.reshape(-1)]
    )
    within_group = lax.psum(local_sums.astype(jnp.bfloat16), "sp").astype(jnp.float32)
    grad_share = lax.psum_scatter(within_group, "dp", scatter_dimension=0, tiled=True)
    edge_cells = inputs.shape[2]
    crop_total = inputs.shape[0] * lax.axis_size("dp")
    norm_factor = 1.0 / jnp.sqrt(jnp.float32(crop_total * edge_cells * edge_cells * edge_cells))
    return (grad_input, grad_share * norm_factor)


def swap_x(value):
    return lax.ppermute(value, "sp", [(0, 1), (1, 0)])


def swap_dp(value, mask, odd_mask=None):
    masks = (mask, mask if odd_mask is None else odd_mask)
    return lax.ppermute(value, "dp", [(i, i ^ masks[i % 2]) for i in range(16)])


def pick(value, dim, index):
    return lax.dynamic_index_in_dim(value, index, dim, keepdims=False)


ORDER = ((1, 3), (2, 1), (3, 2))


def square_sum(pieces, own):
    received = [
        swap_dp(piece, 2 * even, 2 * odd) for piece, (even, odd) in zip(pieces, ORDER)
    ]
    for part in received:
        own += part.astype(jnp.float32)
    return own


def end_sum(square, scale, pieces):
    far = (lax.axis_index("dp") >> 3) & 1
    side = lax.axis_index("sp")
    sent = pick(square, 0, 1 - far).astype(jnp.bfloat16)
    kept = pick(square, 0, far)
    lows, highs = [], []
    received = [swap_dp(sent[first:last], 8) for first, last in pieces]
    for (first, last), part in zip(pieces, received):
        total = (kept[first:last] + part.astype(jnp.float32)).astype(jnp.bfloat16)
        other = swap_x(total)
        lows.append(jnp.where(side == 0, total, other).astype(jnp.float32) * scale)
        highs.append(jnp.where(side == 0, other, total).astype(jnp.float32) * scale)
    return lows, highs


LANES = 128
VMEM = pl.BlockSpec(memory_space=pltpu.VMEM)
BF16, F32 = jnp.bfloat16, jnp.float32
SHARE = 472
HALF = 240
EARLY = 2
PLACES = tuple((i, j, k) for i in range(2) for j in range(2) for k in range(2))


def dot(a, b):
    return jnp.dot(a, b, preferred_element_type=F32)


def against(a, b):
    return lax.dot_general(a, b, (((1,), (1,)), ((), ())), preferred_element_type=F32)


def across(parts):
    return jnp.concatenate(parts, axis=-1)


def split_parity(slab_ref, natural_ref):
    for crop in range(2):
        natural_ref[:, :, 8 * crop : 8 * crop + 8, :] = slab_ref[crop].astype(F32)
    return [natural_ref[:, :, pl.ds(parity, 8, stride=2), :] for parity in range(2)]


def fill_taps(taps_ref, even, odd):
    planes = even.shape[0]
    kk = lax.broadcasted_iota(jnp.int32, even.shape, 2) % 4
    before = jnp.where(kk == 0, 0.0, pltpu.roll(odd, 1, 2))
    after = jnp.where(kk == 3, 0.0, pltpu.roll(even, 7, 2))
    for tap, (low, high) in enumerate(((before, even), (even, odd), (odd, after))):
        taps_ref[1 : 1 + planes, pl.ds(1, 8), :, tap * LANES : (tap + 1) * LANES] = jnp.concatenate(
            [low, high], axis=2
        ).astype(BF16)


def clear_rim(taps_ref, with_planes):
    planes, rows, tile, lanes = taps_ref.shape
    row = jnp.zeros((planes, tile, lanes), BF16)
    taps_ref[:, 0] = row
    taps_ref[:, rows - 1] = row
    if with_planes:
        plane = jnp.zeros((rows, tile, lanes), BF16)
        taps_ref[0] = plane
        taps_ref[planes - 1] = plane


def slab_conv(slab_ref, w_ref, natural_ref, taps_ref):
    even, odd = split_parity(slab_ref, natural_ref)
    clear_rim(taps_ref, False)
    fill_taps(taps_ref, even, odd)
    planes = even.shape[0]
    size = planes * 128
    wide = 3 * LANES
    centre = taps_ref[1 : 1 + planes, 1:9, :, LANES : 2 * LANES].reshape(size, LANES)
    turned = centre.astype(F32).T.astype(BF16)
    cells = across([taps_ref[1 : 1 + planes, j : j + 8].reshape(size, wide) for j in range(3)])

    def weights(i):
        return w_ref[i * 3 * wide : (i + 1) * 3 * wide, :]

    first = dot(cells, across([weights(0), weights(1)])).reshape(planes, 128, 2 * LANES)
    last = dot(cells, weights(2)).reshape(planes, 128, LANES)
    none = jnp.zeros((1, 128, LANES), F32)
    two = jnp.zeros((2, 128, LANES), F32)
    added = (
        jnp.concatenate([two, first[:, :, :LANES]])
        + jnp.concatenate([none, first[:, :, LANES:], none])
        + jnp.concatenate([last, two])
    )
    return added, turned


def blocks(parts, tap):
    i, j, k = PLACES[tap]
    even_odd = parts[k]
    planes = even_odd.shape[0]
    folded = even_odd.reshape(planes // 2, 2, 4, 2, 8, LANES)
    return folded[:, i, :, j].reshape(planes * 16, LANES)


def deep_gradient(parts, w_up_ref):
    upstream = across([blocks(parts, tap).astype(BF16) for tap in range(8)])
    deep = w_up_ref.shape[0] // 8
    w_up = across([w_up_ref[tap * deep : (tap + 1) * deep, :] for tap in range(8)])
    return upstream, against(upstream, w_up)


def own_kernel(in_ref, w_ref, add_ref, turned_ref, natural_ref, taps_ref):
    add_ref[...], turned_ref[...] = slab_conv(in_ref, w_ref, natural_ref, taps_ref)


def forward_kernel(
    in_ref,
    w_ref,
    add_ref,
    turned_own_ref,
    w_down_ref,
    up_ref,
    w_up_ref,
    slope_ref,
    turned_ref,
    hidden_ref,
    act_ref,
    deep_slope_ref,
    blocks_own_ref,
    act_own_ref,
    natural_ref,
    taps_ref,
    sum_ref,
):
    side = lax.axis_index("sp")
    planes = in_ref.shape[1]
    added, turned = slab_conv(in_ref, w_ref, natural_ref, taps_ref)
    sum_ref[...] = jnp.zeros_like(sum_ref)
    sum_ref[pl.ds(side * planes, planes + 2)] = add_ref[...]
    sum_ref[pl.ds((1 - side) * planes, planes + 2)] += added
    turned_ref[side] = turned_own_ref[...]
    turned_ref[1 - side] = turned
    folded = (planes, 2, 4, 2, 2, 8, LANES)
    pre = sum_ref[1 : 1 + 2 * planes].reshape(folded)
    sigmoid_value = jax.nn.sigmoid(pre)
    slope_ref[...] = sigmoid_value * (1.0 + pre * (1.0 - sigmoid_value))
    act = pre * sigmoid_value
    hidden = across([act[:, i, :, j, k].reshape(128, LANES).astype(BF16) for i, j, k in PLACES])
    hidden_ref[...] = hidden.astype(F32).T.astype(BF16)
    pre_deep = dot(hidden, w_down_ref[...])
    act_ref[...] = jax.nn.silu(pre_deep).T.astype(BF16)
    deep_slope_ref[...] = silu_slope(pre_deep)
    blocks_own_ref[...], act_own_ref[...] = deep_gradient(
        split_parity(up_ref, natural_ref), w_up_ref
    )


def backward_kernel(
    up_ref,
    slope_ref,
    turned_ref,
    hidden_ref,
    deep_act_ref,
    deep_slope_ref,
    blocks_own_ref,
    act_own_ref,
    w_down_ref,
    w_up_ref,
    mine_ref,
    first_ref,
    rest_ref,
    taps_ref,
    down_ref,
    natural_ref,
    blocks_ref,
    act_ref,
    folded_ref,
    rows_ref,
):
    side = lax.axis_index("sp")
    core = lax.axis_index("dp") % 2
    parts = split_parity(up_ref, natural_ref)
    upstream, grad_act = deep_gradient(parts, w_up_ref)
    blocks_ref[side] = blocks_own_ref[...]
    blocks_ref[1 - side] = upstream
    act_ref[side] = act_own_ref[...]
    act_ref[1 - side] = grad_act
    upstream = blocks_ref[...].reshape(128, 8 * LANES)
    grad_deep = (act_ref[...].reshape(deep_slope_ref.shape) * deep_slope_ref[...]).astype(BF16)
    back = against(grad_deep, w_down_ref[...]).astype(BF16).astype(F32)
    for tap, (i, j, k) in enumerate(PLACES):
        lanes = slice(tap * LANES, (tap + 1) * LANES)
        summed = (upstream[:, lanes].astype(F32) + back[:, lanes]).reshape(4, 4, 8, LANES)
        folded_ref[:, i, :, j, k] = summed * slope_ref[:, i, :, j, k]
    planes = 8
    whole = (planes, 8, 8, LANES)
    clear_rim(taps_ref, True)
    fill_taps(
        taps_ref,
        folded_ref[:, :, :, :, 0].reshape(whole),
        folded_ref[:, :, :, :, 1].reshape(whole),
    )

    deep = deep_act_ref.shape[0]
    grad_up = dot(deep_act_ref[...], upstream)
    down_at = 27 * LANES
    up_at = down_at + 8 * deep
    for tap in range(8):
        rows_ref[up_at + tap * deep : up_at + (tap + 1) * deep, :] = grad_up[
            :, tap * LANES : (tap + 1) * LANES
        ]
    grad_down = dot(hidden_ref[...], grad_deep)
    for part in range(deep // LANES):
        rows_ref[pl.ds(down_at + part, 8 * LANES, stride=deep // LANES), :] = grad_down[
            :, part * LANES : (part + 1) * LANES
        ]
    down_ref[...] = rows_ref[down_at : down_at + down_ref.shape[0], :]
    here = (lax.axis_index("dp") >> 1) & 3

    def give(own_side, other):
        conv_rows(own_side, other, turned_ref, taps_ref, rows_ref)
        steps = [step[other] for step in ORDER] + [0]
        for far in range(2):
            for place, step in enumerate(steps):
                start = window(own_side, other, 4 * far + (here ^ step))
                target, slot = (first_ref, place) if place < EARLY else (rest_ref, place - EARLY)
                target[2 * slot + far] = rows_ref[
                    pl.ds(pl.multiple_of(start, 8), HALF), :
                ].astype(BF16)
        keep_rows(own_side, 1 - other, range(4, 8), rows_ref, mine_ref)

    for_place(side, 1 - core, give)


def for_place(side, owner, body):
    for own_side in range(2):
        for own_owner in range(2):
            pl.when((side == own_side) & (owner == own_owner))(
                functools.partial(body, own_side, own_owner)
            )


def window(side, owner, pair):
    return (2 * pair + owner) * SHARE + side * (SHARE - HALF)


def conv_rows(side, owner, turned_ref, taps_ref, rows_ref):
    starts = [window(side, owner, pair) for pair in range(8)]
    kept = [
        tap
        for tap in range(27)
        if any(at < (tap + 1) * LANES and tap * LANES < at + HALF for at in starts)
    ]
    turned = across([turned_ref[0], turned_ref[1]])
    planes = taps_ref.shape[0] - 2
    size = planes * 128
    cells = []
    for tap in kept:
        i, j, k = (26 - tap) // 9, (26 - tap) // 3 % 3, (26 - tap) % 3
        cells.append(
            taps_ref[i : i + planes, j : j + 8, :, k * LANES : (k + 1) * LANES].reshape(size, LANES)
        )
    sums = dot(turned, across(cells))
    for at, tap in enumerate(kept):
        rows_ref[tap * LANES : (tap + 1) * LANES, :] = sums[:, at * LANES : (at + 1) * LANES]


def keep_rows(side, owner, pairs, rows_ref, target_ref):
    for at, pair in enumerate(pairs):
        first = window(side, owner, pair)
        target_ref[at] = rows_ref[first : first + HALF, :].astype(BF16)


def own_rows_kernel(taps_ref, turned_ref, down_ref, mine_ref, rows_ref):
    rows_ref[27 * LANES :, :] = down_ref[...]

    def give(own_side, own_core):
        conv_rows(own_side, own_core, turned_ref, taps_ref, rows_ref)
        keep_rows(own_side, own_core, range(4), rows_ref, mine_ref)

    for_place(lax.axis_index("sp"), lax.axis_index("dp") % 2, give)


def chip_kernel(steps, late_ref, early_ref, passed_ref, *targets):
    at = lax.axis_index("dp")
    for place, ((even, odd), target) in enumerate(zip(steps, targets)):
        index = ((at >> 1) & 3) ^ (even + (at & 1) * (odd - even))
        for far, mine_ref in enumerate((late_ref, early_ref)):
            total = mine_ref[index].astype(F32) + passed_ref[2 * place + far].astype(F32)
            target[far] = total.astype(target.dtype)


def input_kernel(taps_ref, w_ref, out_ref, natural_ref):
    own = out_ref.shape[1]
    size = own * 128
    first_plane = lax.axis_index("sp") * own
    total = jnp.zeros((size, LANES), F32)
    for i in range(3):
        for j in range(3):
            first = 26 - 9 * i - 3 * j
            weights = across(
                [w_ref[(first - k) * LANES : (first - k + 1) * LANES, :] for k in range(3)]
            )
            cells = taps_ref[pl.ds(first_plane + i, own), j : j + 8].reshape(size, 3 * LANES)
            total += against(cells, weights)
    total = total.reshape(own, 8, 2, 8, LANES)
    for parity in range(2):
        natural_ref[:, :, pl.ds(parity, 8, stride=2), :] = total[:, :, parity]
    for crop in range(2):
        out_ref[crop] = natural_ref[:, :, 8 * crop : 8 * crop + 8, :].astype(BF16)


def run(body, operands, outs, scratch, flops):
    return pl.pallas_call(
        body,
        out_shape=tuple(jax.ShapeDtypeStruct(shape, kind) for shape, kind in outs),
        in_specs=[VMEM] * len(operands),
        out_specs=(VMEM,) * len(outs),
        scratch_shapes=[pltpu.VMEM(shape, kind) for shape, kind in scratch],
        compiler_params=pltpu.CompilerParams(vmem_limit_bytes=24 << 20),
        cost_estimate=pl.CostEstimate(flops=flops, bytes_accessed=1 << 21, transcendentals=0),
    )(*operands)


def per_device_pairs(inputs, cotangent, w_conv, w_down, w_up):
    deep = w_down.shape[1]
    other_in = swap_x(inputs)
    other_up = swap_x(cotangent)
    natural = ((4, 8, 16, LANES), F32)
    slab_taps = ((6, 10, 16, 3 * LANES), BF16)
    blocked = ((64, 8 * LANES), BF16)
    act = ((64, deep), F32)
    added, turned_own = run(
        own_kernel,
        (inputs, w_conv),
        [((6, 128, LANES), F32), ((LANES, 512), BF16)],
        [natural, slab_taps],
        10**9,
    )
    folded = ((4, 2, 4, 2, 2, 8, LANES), F32)
    saved = run(
        forward_kernel,
        (other_in, w_conv, added, turned_own, w_down, cotangent, w_up),
        [
            folded,
            ((2, LANES, 512), BF16),
            ((8 * LANES, 128), BF16),
            ((deep, 128), BF16),
            ((128, deep), F32),
            blocked,
            act,
        ],
        [natural, slab_taps, ((10, 128, LANES), F32)],
        10**9,
    )
    total_rows = (w_conv.size + w_down.size + w_up.size) // LANES
    conv_count = w_conv.size // LANES
    taps = ((10, 10, 16, 3 * LANES), BF16)
    given = ((4, HALF, LANES), BF16)
    down = ((8 * SHARE - conv_count, LANES), F32)
    early_mine, first, rest, grad_taps, down_rows = run(
        backward_kernel,
        (other_up, *saved, w_down, w_up),
        [
            given,
            ((2 * EARLY, HALF, LANES), BF16),
            ((8 - 2 * EARLY, HALF, LANES), BF16),
            taps,
            down,
        ],
        [
            natural,
            ((2, *blocked[0]), BF16),
            ((2, *act[0]), F32),
            folded,
            ((total_rows, LANES), F32),
        ],
        10**9,
    )
    (late_mine,) = run(
        own_rows_kernel,
        (grad_taps, saved[1], down_rows),
        [given],
        [((8 * SHARE, LANES), F32)],
        10**9,
    )
    (grad_input,) = run(
        input_kernel,
        (grad_taps, w_conv),
        [(inputs.shape, BF16)],
        [natural],
        10**9,
    )

    first, rest = swap_dp(first, 1), swap_dp(rest, 1)
    sums = [((2, HALF, LANES), BF16)] * 3 + [((2, HALF, LANES), F32)]
    steps = (*ORDER, (0, 0))
    *pieces, own = (
        part
        for passed, places in ((first, slice(0, EARLY)), (rest, slice(EARLY, 4)))
        for part in run(
            functools.partial(chip_kernel, steps[places]),
            (late_mine, early_mine, passed),
            sums[places],
            [],
            10**6,
        )
    )
    square = square_sum(pieces, own)
    crop_total = inputs.shape[0] * lax.axis_size("dp")
    scale = 1.0 / jnp.sqrt(jnp.float32(crop_total * inputs.shape[2] ** 3))
    lows, highs = end_sum(square, scale, ((0, HALF),))
    highs[0] = highs[0][2 * HALF - SHARE :]
    grad_share = jnp.concatenate(lows + highs).reshape(-1)
    return (grad_input, grad_share)


def solution(mesh):
    pairs = dict(mesh.shape) == {"sp": 2, "dp": 16}
    return jax.shard_map(
        per_device_pairs if pairs else per_device,
        mesh=mesh,
        in_specs=(P("dp", "sp", None, None, None), P("dp", "sp", None, None, None), P(), P(), P()),
        out_specs=(P("dp", "sp", None, None, None), P("dp")),
        check_vma=False,
    )
```
